128 devices in a mesh: row: 32 (over x, z, core), col: 4 (over y).
Axes of the slice: x: 4, y: 4, z: 4, core: 2. Of those that a mesh axis runs over, the one named last changes fastest.
Arguments:
- grad_joined: bfloat16 [48, 1024, 1024], P(None, 'row', 'col'), may hold values from -6 to 6
- joined_fine: bfloat16 [48, 1024, 1024], P(None, 'row', 'col'), as said below
- input_fine: bfloat16 [48, 1024, 1024], P(None, 'row', 'col'), may hold values from -6 to 6
- inner_fine: bfloat16 [48, 1024, 1024], P(None, 'row', 'col'), as said below
- unit_fine: bfloat16 [48, 1024, 1024], P(None, 'row', 'col'), as said below
- input_mid: bfloat16 [96, 512, 512], P(None, 'row', 'col'), may hold values from -6 to 6
- inner_mid: bfloat16 [96, 512, 512], P(None, 'row', 'col'), as said below
- unit_mid: bfloat16 [96, 512, 512], P(None, 'row', 'col'), as said below
- input_coarse: bfloat16 [192, 256, 256], P(None, 'row', 'col'), may hold values from -6 to 6
- inner_coarse: bfloat16 [192, 256, 256], P(None, 'row', 'col'), as said below
- unit_coarse: bfloat16 [192, 256, 256], P(None, 'row', 'col'), as said below
- first_fine: bfloat16 [3, 3, 48, 48], replicated, may hold values from -0.3125 to 0.3125
- second_fine: bfloat16 [3, 3, 48, 48], replicated, may hold values from -0.3125 to 0.3125
- first_mid: bfloat16 [3, 3, 96, 96], replicated, may hold values from -0.21875 to 0.21875
- second_mid: bfloat16 [3, 3, 96, 96], replicated, may hold values from -0.21875 to 0.21875
- first_coarse: bfloat16 [3, 3, 192, 192], replicated, may hold values from -0.15625 to 0.15625
- second_coarse: bfloat16 [3, 3, 192, 192], replicated, may hold values from -0.15625 to 0.15625
- lift_mid: bfloat16 [96, 48], replicated, may hold values from -0.625 to 0.625
- lift_coarse: bfloat16 [192, 48], replicated, may hold values from -0.4375 to 0.4375
Outputs:
- grad_input_fine: bfloat16 [48, 1024, 1024], P(None, 'row', 'col')
- grad_input_mid: bfloat16 [96, 512, 512], P(None, 'row', 'col')
- grad_input_coarse: bfloat16 [192, 256, 256], P(None, 'row', 'col')
- grad_first_fine: float32 [3, 3, 48, 48], replicated
- grad_second_fine: float32 [3, 3, 48, 48], replicated
- grad_first_mid: float32 [3, 3, 96, 96], replicated
- grad_second_mid: float32 [3, 3, 96, 96], replicated
- grad_first_coarse: float32 [3, 3, 192, 192], replicated
- grad_second_coarse: float32 [3, 3, 192, 192], replicated
- grad_lift_mid: float32 [96, 48], replicated
- grad_lift_coarse: float32 [192, 48], replicated
The draws below stay inside these ranges and needn't reach their ends.
Inputs may be any that keep to these rules, and one draw needn't show every extreme that they name: `joined_fine`: saved ReLU outputs. `inner_fine`: saved ReLU outputs. `unit_fine`: saved ReLU outputs. `inner_mid`: saved ReLU outputs. `unit_mid`: saved ReLU outputs. `inner_coarse`: saved ReLU outputs. `unit_coarse`: saved ReLU outputs.
All inputs are finite; a program needn't handle non-finite values.
Results may differ from the reference program's by a relative error of at most 0.015.
Values may be sent and summed in bfloat16 or wider, within the bound.
No kernel may reach another device: no remote copies, remote signals or barrier semaphores. Data moves between devices by JAX's collectives and lax.ppermute only.
A program may use at most 128 MiB of HBM per device.

```python
import jax
import jax.numpy as jnp

C1 = 48
C2 = 96
C3 = 192
H1 = 1024
W1 = 1024
H2 = 512
W2 = 512
H3 = 256
W3 = 256


def rectified_normal(key, shape):
    return jnp.maximum(jax.random.normal(key, shape, jnp.float32), 0.0).astype(jnp.bfloat16)


def draw_joined_fine(key, part):
    key = jax.random.fold_in(key, 11)
    return rectified_normal(key, (C1, H1, W1))


def draw_inner_fine(key, part):
    key = jax.random.fold_in(key, 12)
    return rectified_normal(key, (C1, H1, W1))


def draw_unit_fine(key, part):
    key = jax.random.fold_in(key, 13)
    return rectified_normal(key, (C1, H1, W1))


def draw_inner_mid(key, part):
    key = jax.random.fold_in(key, 14)
    return rectified_normal(key, (C2, H2, W2))


def draw_unit_mid(key, part):
    key = jax.random.fold_in(key, 15)
    return rectified_normal(key, (C2, H2, W2))


def draw_inner_coarse(key, part):
    key = jax.random.fold_in(key, 16)
    return rectified_normal(key, (C3, H3, W3))


def draw_unit_coarse(key, part):
    key = jax.random.fold_in(key, 17)
    return rectified_normal(key, (C3, H3, W3))


def steps_of(key, dims, shards, low, high):
    loudness, own = 1.0, jax.random.fold_in(key, 6)
    for axis_at, blocks in shards:
        heights = jnp.exp(jax.random.uniform(jax.random.fold_in(own, axis_at), (blocks,), jnp.float32, low / len(shards), high / len(shards)))
        loudness = loudness * jnp.repeat(heights, dims[axis_at] // blocks).reshape([-1 if axis == axis_at else 1 for axis in range(len(dims))])
    return loudness


def gaussian(stream_key, shape, spread, limit, cuts=(), dtype=jnp.bfloat16):
    level = steps_of(stream_key, shape, cuts, -0.22, 0.18) if cuts else 1.0
    entries = jax.random.normal(stream_key, shape, jnp.float32) * spread * level
    return jnp.minimum(jnp.maximum(entries, -limit), limit).astype(dtype)


def setup_inputs(seed: int = 0) -> dict:
    keys = jax.random.split(jax.random.key(seed), 20)
    grad_joined = gaussian(keys[0], (C1, H1, W1), 1.0, 6.0, ((1, 32), (2, 4)))
    joined_fine = draw_joined_fine(jax.random.fold_in(keys[19], 71), 0)
    input_fine = gaussian(keys[2], (C1, H1, W1), 1.0, 6.0, ((1, 32), (2, 4)))
    inner_fine = draw_inner_fine(jax.random.fold_in(keys[19], 71), 0)
    unit_fine = draw_unit_fine(jax.random.fold_in(keys[19], 71), 0)
    input_mid = gaussian(keys[5], (C2, H2, W2), 1.0, 6.0, ((1, 32), (2, 4)))
    inner_mid = draw_inner_mid(jax.random.fold_in(keys[19], 71), 0)
    unit_mid = draw_unit_mid(jax.random.fold_in(keys[19], 71), 0)
    input_coarse = gaussian(keys[8], (C3, H3, W3), 1.0, 6.0, ((1, 32), (2, 4)))
    inner_coarse = draw_inner_coarse(jax.random.fold_in(keys[19], 71), 0)
    unit_coarse = draw_unit_coarse(jax.random.fold_in(keys[19], 71), 0)
    first_fine = gaussian(keys[11], (3, 3, C1, C1), (9 * C1) ** -0.5, 0.3125)
    second_fine = gaussian(keys[12], (3, 3, C1, C1), (9 * C1) ** -0.5, 0.3125)
    first_mid = gaussian(keys[13], (3, 3, C2, C2), (9 * C2) ** -0.5, 0.21875)
    second_mid = gaussian(keys[14], (3, 3, C2, C2), (9 * C2) ** -0.5, 0.21875)
    first_coarse = gaussian(keys[15], (3, 3, C3, C3), (9 * C3) ** -0.5, 0.15625)
    second_coarse = gaussian(keys[16], (3, 3, C3, C3), (9 * C3) ** -0.5, 0.15625)
    lift_mid = gaussian(keys[17], (C2, C1), C2 ** -0.5, 0.625)
    lift_coarse = gaussian(keys[18], (C3, C1), C3 ** -0.5, 0.4375)
    return dict(grad_joined=grad_joined, joined_fine=joined_fine, input_fine=input_fine, inner_fine=inner_fine, unit_fine=unit_fine, input_mid=input_mid, inner_mid=inner_mid, unit_mid=unit_mid, input_coarse=input_coarse, inner_coarse=inner_coarse, unit_coarse=unit_coarse, first_fine=first_fine, second_fine=second_fine, first_mid=first_mid, second_mid=second_mid, first_coarse=first_coarse, second_coarse=second_coarse, lift_mid=lift_mid, lift_coarse=lift_coarse)


def pad_grid(tile):
    return jnp.pad(tile, ((0, 0), (1, 1), (1, 1)))


def tap_sum(padded, weight, row_count, col_count):
    padded = padded.astype(jnp.float32)
    total = jnp.zeros((weight.shape[2], row_count, col_count), jnp.float32)
    for row_tap in range(3):
        for col_tap in range(3):
            window = padded[:, 2 - row_tap:2 - row_tap + row_count, 2 - col_tap:2 - col_tap + col_count]
            total = total + jnp.einsum("io,ohw->ihw", weight[row_tap, col_tap].astype(jnp.float32), window)
    return total


def tap_corr(source, padded):
    row_count, col_count = source.shape[1], source.shape[2]
    source = source.astype(jnp.float32)
    padded = padded.astype(jnp.float32)
    outer = []
    for row_tap in range(3):
        inner_list = []
        for col_tap in range(3):
            window = padded[:, 2 - row_tap:2 - row_tap + row_count, 2 - col_tap:2 - col_tap + col_count]
            inner_list.append(jnp.einsum("ihw,ohw->io", source, window))
        outer.append(jnp.stack(inner_list))
    return jnp.stack(outer)


def unit_backward(source, inner, result, upstream, first, second):
    masked = jnp.where(result > 0, upstream, jnp.zeros_like(upstream))
    row_count, col_count = masked.shape[1], masked.shape[2]
    grad_padded = pad_grid(masked)
    inner_grad = tap_sum(grad_padded, second, row_count, col_count)
    pre_grad = jnp.where(inner > 0, inner_grad, jnp.zeros_like(inner_grad)).astype(jnp.bfloat16)
    pre_padded = pad_grid(pre_grad)
    grad_source = masked.astype(jnp.float32) + tap_sum(pre_padded, first, row_count, col_count)
    return grad_source.astype(jnp.bfloat16), tap_corr(source, pre_padded), tap_corr(inner, grad_padded)


def block_pool(tile, factor):
    channels, row_count, col_count = tile.shape
    shaped = tile.astype(jnp.float32).reshape(channels, row_count // factor, factor, col_count // factor, factor)
    return shaped.sum(axis=(2, 4)).astype(jnp.bfloat16)


def reference(grad_joined, joined_fine, input_fine, inner_fine, unit_fine, input_mid, inner_mid, unit_mid,
              input_coarse, inner_coarse, unit_coarse, first_fine, second_fine, first_mid, second_mid,
              first_coarse, second_coarse, lift_mid, lift_coarse):
    upstream = jnp.where(joined_fine > 0, grad_joined, jnp.zeros_like(grad_joined))
    pooled_mid = block_pool(upstream, 2)
    pooled_coarse = block_pool(upstream, 4)
    grad_unit_mid = jnp.einsum("kc,chw->khw", lift_mid.astype(jnp.float32), pooled_mid.astype(jnp.float32)).astype(jnp.bfloat16)
    grad_unit_coarse = jnp.einsum("kc,chw->khw", lift_coarse.astype(jnp.float32), pooled_coarse.astype(jnp.float32)).astype(jnp.bfloat16)
    grad_lift_mid = jnp.einsum("khw,chw->kc", unit_mid.astype(jnp.float32), pooled_mid.astype(jnp.float32))
    grad_lift_coarse = jnp.einsum("khw,chw->kc", unit_coarse.astype(jnp.float32), pooled_coarse.astype(jnp.float32))
    fine_input, fine_first, fine_second = unit_backward(input_fine, inner_fine, unit_fine, upstream, first_fine, second_fine)
    mid_input, mid_first, mid_second = unit_backward(input_mid, inner_mid, unit_mid, grad_unit_mid, first_mid, second_mid)
    coarse_input, coarse_first, coarse_second = unit_backward(input_coarse, inner_coarse, unit_coarse, grad_unit_coarse, first_coarse, second_coarse)
    return (fine_input, mid_input, coarse_input, fine_first, fine_second, mid_first, mid_second,
            coarse_first, coarse_second, grad_lift_mid, grad_lift_coarse)
```

```python
import jax
import jax.numpy as jnp
from jax import lax
from jax.sharding import PartitionSpec as P


AXES = ("row", "col")
ORDER = (("y", "x", "z"), ("x", "z", "y"))
CORE_PAIRS = [(d, d ^ 4) for d in range(128)]


def stage_pairs(stage, k):
    pairs = []
    for d in range(128):
        row, col = divmod(d, 4)
        at = {"x": row // 8, "z": (row // 2) % 4, "y": col}
        core = row % 2
        at[ORDER[core][stage]] ^= k
        pairs.append((d, (at["x"] * 8 + at["z"] * 2 + core) * 4 + at["y"]))
    return pairs


def my_place():
    row, col = lax.axis_index("row"), lax.axis_index("col")
    at = {"x": row // 8, "z": (row // 2) % 4, "y": col}
    core = row % 2
    return core, [jnp.where(core == 0, at[ORDER[0][s]], at[ORDER[1][s]]) for s in range(3)]


def send(block, pairs):
    return lax.ppermute(block, AXES, pairs)


def add4(own, others):
    a, b, c = [other.astype(jnp.float32) for other in others]
    return ((own.astype(jnp.float32) + a) + (b + c)).astype(jnp.bfloat16)


def scatter_stage(block, stage, mine):
    parts = block.reshape(4, block.shape[0] // 4, block.shape[1])
    own = lax.dynamic_index_in_dim(parts, mine, 0, keepdims=False)
    others = [
        send(lax.dynamic_index_in_dim(parts, mine ^ k, 0, keepdims=False), stage_pairs(stage, k))
        for k in (1, 2, 3)
    ]
    return add4(own, others)


def reduce_stage(block, stage):
    return add4(block, [send(block, stage_pairs(stage, k)) for k in (1, 2, 3)])


def gather_stage(block, stage, mine):
    parts = [block] + [send(block, stage_pairs(stage, k)) for k in (1, 2, 3)]
    whole = jnp.zeros((4,) + block.shape, block.dtype)
    for k in range(4):
        whole = lax.dynamic_update_index_in_dim(whole, parts[k], mine ^ k, 0)
    return whole.reshape(4 * block.shape[0], block.shape[1])


def all_sum(block):
    core, mine = my_place()
    half = block.shape[0] // 2
    halves = block.reshape(2, half, block.shape[1])
    other = send(lax.dynamic_index_in_dim(halves, 1 - core, 0, keepdims=False), CORE_PAIRS)
    own = lax.dynamic_index_in_dim(halves, core, 0, keepdims=False)
    part = (own.astype(jnp.float32) + other.astype(jnp.float32)).astype(jnp.bfloat16)
    part = scatter_stage(part, 0, mine[0])
    part = scatter_stage(part, 1, mine[1])
    part = reduce_stage(part, 2)
    part = gather_stage(part, 1, mine[1])
    part = gather_stage(part, 0, mine[0])
    other = send(part, CORE_PAIRS)
    return jnp.where(core == 0, jnp.concatenate([part, other]), jnp.concatenate([other, part]))


def pack(grads):
    flat = [g.astype(jnp.bfloat16).reshape(-1) for g in grads]
    size = sum(g.shape[0] for g in flat)
    rows = -(-size // (128 * 32 * 16)) * 32 * 16
    flat.append(jnp.zeros((rows * 128 - size,), jnp.bfloat16))
    return jnp.concatenate(flat).reshape(rows, 128)


def unpack(block, grads):
    flat = block.reshape(-1).astype(jnp.float32)
    out, at = [], 0
    for g in grads:
        out.append(flat[at : at + g.size].reshape(g.shape))
        at += g.size
    return out


def sum_grads(grads):
    return unpack(all_sum(pack(grads)), grads)


def with_halo(block, sides, width):
    for axis, dim in sides:
        count = lax.axis_size(axis)
        forward = [(i, i + 1) for i in range(count - 1)]
        backward = [(target, source) for source, target in forward]
        low = lax.ppermute(
            lax.slice_in_dim(block, block.shape[dim] - width, None, axis=dim), axis, forward
        )
        high = lax.ppermute(lax.slice_in_dim(block, 0, width, axis=dim), axis, backward)
        block = jnp.concatenate([low, block, high], axis=dim)
    return block


def tap_sum(padded, weight, row_count, col_count):
    total = jnp.zeros((weight.shape[2], row_count, col_count), jnp.float32)
    for row_tap in range(3):
        for col_tap in range(3):
            window = padded[
                :, 2 - row_tap : 2 - row_tap + row_count, 2 - col_tap : 2 - col_tap + col_count
            ]
            total = total + jnp.einsum(
                "io,ohw->ihw", weight[row_tap, col_tap], window, preferred_element_type=jnp.float32
            )
    return total


def tap_corr(source, padded):
    row_count, col_count = (source.shape[1], source.shape[2])
    outer = []
    for row_tap in range(3):
        inner_list = []
        for col_tap in range(3):
            window = padded[
                :, 2 - row_tap : 2 - row_tap + row_count, 2 - col_tap : 2 - col_tap + col_count
            ]
            inner_list.append(
                jnp.einsum("ihw,ohw->io", source, window, preferred_element_type=jnp.float32)
            )
        outer.append(jnp.stack(inner_list))
    return jnp.stack(outer)


def fine_grad_rims(tile, width):
    return with_halo(tile, (("row", 1), ("col", 2)), width)


def fine_inner_rims(tile):
    return with_halo(tile, (("row", 1), ("col", 2)), 1)


def unit_backward(source, inner, result, upstream, first, second, pad_grad, pad_inner):
    masked = jnp.where(result > 0, upstream, jnp.zeros_like(upstream))
    row_count, col_count = (masked.shape[1], masked.shape[2])
    grad_padded = pad_grad(masked, 1)
    inner_grad = tap_sum(grad_padded, second, row_count, col_count)
    pre_grad = jnp.where(inner > 0, inner_grad, jnp.zeros_like(inner_grad)).astype(jnp.bfloat16)
    pre_padded = pad_inner(pre_grad)
    grad_source = masked.astype(jnp.float32) + tap_sum(pre_padded, first, row_count, col_count)
    return (
        grad_source.astype(jnp.bfloat16),
        tap_corr(source, pre_padded),
        tap_corr(inner, grad_padded),
    )


def block_pool(tile, factor):
    channels, row_count, col_count = tile.shape
    column_ids = lax.broadcasted_iota(jnp.int32, (col_count, col_count // factor), 0) // factor
    target_ids = lax.broadcasted_iota(jnp.int32, (col_count, col_count // factor), 1)
    pooling = (column_ids == target_ids).astype(jnp.bfloat16)
    summed = jnp.einsum("chw,wv->chv", tile, pooling, preferred_element_type=jnp.float32)
    summed = summed.reshape(channels, row_count // factor, factor, col_count // factor).sum(axis=2)
    return summed.astype(jnp.bfloat16)


def on_device(
    grad_joined,
    joined_fine,
    input_fine,
    inner_fine,
    unit_fine,
    input_mid,
    inner_mid,
    unit_mid,
    input_coarse,
    inner_coarse,
    unit_coarse,
    first_fine,
    second_fine,
    first_mid,
    second_mid,
    first_coarse,
    second_coarse,
    lift_mid,
    lift_coarse,
):
    upstream = jnp.where(joined_fine > 0, grad_joined, jnp.zeros_like(grad_joined))
    pooled_mid = block_pool(upstream, 2)
    pooled_coarse = block_pool(upstream, 4)
    grad_unit_mid = jnp.einsum(
        "kc,chw->khw", lift_mid, pooled_mid, preferred_element_type=jnp.float32
    ).astype(jnp.bfloat16)
    grad_unit_coarse = jnp.einsum(
        "kc,chw->khw", lift_coarse, pooled_coarse, preferred_element_type=jnp.float32
    ).astype(jnp.bfloat16)
    grad_lift_mid = jnp.einsum(
        "khw,chw->kc", unit_mid, pooled_mid, preferred_element_type=jnp.float32
    )
    grad_lift_coarse = jnp.einsum(
        "khw,chw->kc", unit_coarse, pooled_coarse, preferred_element_type=jnp.float32
    )
    fine_input, fine_first, fine_second = unit_backward(
        input_fine,
        inner_fine,
        unit_fine,
        upstream,
        first_fine,
        second_fine,
        fine_grad_rims,
        fine_inner_rims,
    )
    mid_input, mid_first, mid_second = unit_backward(
        input_mid,
        inner_mid,
        unit_mid,
        grad_unit_mid,
        first_mid,
        second_mid,
        fine_grad_rims,
        fine_inner_rims,
    )
    coarse_input, coarse_first, coarse_second = unit_backward(
        input_coarse,
        inner_coarse,
        unit_coarse,
        grad_unit_coarse,
        first_coarse,
        second_coarse,
        fine_grad_rims,
        fine_inner_rims,
    )
    (
        fine_first,
        fine_second,
        mid_first,
        mid_second,
        coarse_first,
        coarse_second,
        grad_lift_mid,
        grad_lift_coarse,
    ) = sum_grads(
        (
            fine_first,
            fine_second,
            mid_first,
            mid_second,
            coarse_first,
            coarse_second,
            grad_lift_mid,
            grad_lift_coarse,
        )
    )
    return (
        fine_input,
        mid_input,
        coarse_input,
        fine_first,
        fine_second,
        mid_first,
        mid_second,
        coarse_first,
        coarse_second,
        grad_lift_mid,
        grad_lift_coarse,
    )


def solution(mesh):
    in_specs = (
        P(None, "row", "col"),
        P(None, "row", "col"),
        P(None, "row", "col"),
        P(None, "row", "col"),
        P(None, "row", "col"),
        P(None, "row", "col"),
        P(None, "row", "col"),
        P(None, "row", "col"),
        P(None, "row", "col"),
        P(None, "row", "col"),
        P(None, "row", "col"),
        P(),
        P(),
        P(),
        P(),
        P(),
        P(),
        P(),
        P(),
    )
    out_specs = (
        P(None, "row", "col"),
        P(None, "row", "col"),
        P(None, "row", "col"),
        P(),
        P(),
        P(),
        P(),
        P(),
        P(),
        P(),
        P(),
    )
    return jax.shard_map(
        on_device, mesh=mesh, in_specs=in_specs, out_specs=out_specs, check_vma=False
    )
```

```python
import jax
import jax.numpy as jnp
import numpy as np
from jax import lax
from jax.experimental import pallas as pl
from jax.experimental.pallas import tpu as pltpu
from jax.sharding import PartitionSpec as P

ROWS, COLS = 32, 4
CELLS = 1536
FINE, MID = 48, 96
COARSE_ROWS, COARSE_COLS, COARSE = 8, 64, 192
PITCH = 80
PARAMS = pltpu.CompilerParams(vmem_limit_bytes=56 * 2**20)

AXES = ("row", "col")
ORDER = (("y", "x", "z"), ("x", "z", "y"))
CORE_PAIRS = [(d, d ^ 4) for d in range(128)]


def stage_pairs(stage, k):
    pairs = []
    for d in range(128):
        row, col = divmod(d, 4)
        at = {"x": row // 8, "z": (row // 2) % 4, "y": col}
        core = row % 2
        at[ORDER[core][stage]] ^= k
        pairs.append((d, (at["x"] * 8 + at["z"] * 2 + core) * 4 + at["y"]))
    return pairs


def my_place():
    row, col = lax.axis_index("row"), lax.axis_index("col")
    at = {"x": row // 8, "z": (row // 2) % 4, "y": col}
    core = row % 2
    return core, [jnp.where(core == 0, at[ORDER[0][s]], at[ORDER[1][s]]) for s in range(3)]


def send(block, pairs):
    return lax.ppermute(block, AXES, pairs)


def add4(own, others):
    a, b, c = [other.astype(jnp.float32) for other in others]
    return ((own.astype(jnp.float32) + a) + (b + c)).astype(jnp.bfloat16)


def scatter_stage(block, stage, mine):
    parts = block.reshape(4, block.shape[0] // 4, block.shape[1])
    own = lax.dynamic_index_in_dim(parts, mine, 0, keepdims=False)
    others = [
        send(lax.dynamic_index_in_dim(parts, mine ^ k, 0, keepdims=False), stage_pairs(stage, k))
        for k in (1, 2, 3)
    ]
    return add4(own, others)


def reduce_stage(block, stage):
    return add4(block, [send(block, stage_pairs(stage, k)) for k in (1, 2, 3)])


def gather_stage(block, stage, mine):
    parts = [block] + [send(block, stage_pairs(stage, k)) for k in (1, 2, 3)]
    whole = jnp.zeros((4,) + block.shape, block.dtype)
    for k in range(4):
        whole = lax.dynamic_update_index_in_dim(whole, parts[k], mine ^ k, 0)
    return whole.reshape(4 * block.shape[0], block.shape[1])


def all_sum(block):
    core, mine = my_place()
    half = block.shape[0] // 2
    halves = block.reshape(2, half, block.shape[1])
    other = send(lax.dynamic_index_in_dim(halves, 1 - core, 0, keepdims=False), CORE_PAIRS)
    own = lax.dynamic_index_in_dim(halves, core, 0, keepdims=False)
    part = (own.astype(jnp.float32) + other.astype(jnp.float32)).astype(jnp.bfloat16)
    part = scatter_stage(part, 0, mine[0])
    part = scatter_stage(part, 1, mine[1])
    part = reduce_stage(part, 2)
    part = gather_stage(part, 1, mine[1])
    part = gather_stage(part, 0, mine[0])
    other = send(part, CORE_PAIRS)
    return jnp.where(core == 0, jnp.concatenate([part, other]), jnp.concatenate([other, part]))


def shift_pairs(down, right):
    return [
        (row * COLS + col, (row + down) * COLS + col + right)
        for row in range(ROWS)
        for col in range(COLS)
        if 0 <= row + down < ROWS and 0 <= col + right < COLS
    ]


def iota(shape, dim):
    return lax.broadcasted_iota(jnp.int32, shape, dim)


def picks(shape, pairs):
    rows, cols = iota(shape, 0), iota(shape, 1)
    hit = jnp.zeros(shape, jnp.bool_)
    for row, col in pairs:
        hit = hit | ((rows == row) & (cols == col))
    return hit.astype(jnp.float32).astype(jnp.bfloat16)


def dot(a, b, a_dim=1, b_dim=0):
    return lax.dot_general(
        a, b, (((a_dim,), (b_dim,)), ((), ())), preferred_element_type=jnp.float32
    )


def keep(gate, value):
    return jnp.where(gate > 0, value, jnp.zeros_like(value))


def prep_kernel(
    grad, joined, unit_fine, inner_fine, unit_mid, inner_mid, unit_coarse, inner_coarse, lift_mid, lift_coarse,
    fine, mid, coarse, up, down, left, right, lift, upstream, gate_mid, in_fine, in_mid,
):
    above = keep(joined[...], grad[...])
    upstream[...] = jnp.transpose(above, (1, 0, 2)).reshape(CELLS, 256)
    fine[...] = jnp.transpose(keep(unit_fine[...], above), (1, 0, 2)).reshape(CELLS, 256)
    gate_mid[...] = jnp.transpose(unit_mid[...], (1, 0, 2)).reshape(CELLS, 128)
    in_fine[...] = jnp.transpose(inner_fine[...], (1, 0, 2)).reshape(CELLS, 256)
    in_mid[...] = jnp.transpose(inner_mid[...], (1, 0, 2)).reshape(CELLS, 128)

    cells, target = iota((256, 192), 0), iota((256, 192), 1)
    pooling = jnp.where(target < 128, cells // 2, cells // 4 + 128) == target
    pooling = pooling.astype(jnp.float32).astype(jnp.bfloat16)
    sum_mid = jnp.zeros((MID, FINE), jnp.float32)
    sum_coarse = jnp.zeros((FINE, COARSE), jnp.float32)
    for row in range(COARSE_ROWS):
        pooled = dot(upstream[row * 192 : (row + 1) * 192, :], pooling)
        quarter = [pooled[k * FINE : (k + 1) * FINE] for k in range(4)]
        for half in range(2):
            cell = (quarter[2 * half] + quarter[2 * half + 1])[:, :128].astype(jnp.bfloat16)
            rows = slice((2 * row + half) * MID, (2 * row + half + 1) * MID)
            gate = gate_mid[rows, :]
            mid[rows, :] = keep(gate, dot(lift_mid[...], cell).astype(jnp.bfloat16))
            sum_mid += dot(gate, cell, 1, 1)
        cell = ((quarter[0] + quarter[1]) + (quarter[2] + quarter[3]))[:, 128:].astype(jnp.bfloat16)
        gate = unit_coarse[row]
        coarse[row] = keep(gate, dot(cell, lift_coarse[...], 0, 1).astype(jnp.bfloat16))
        sum_coarse += dot(cell, gate)

    lift[...] = jnp.zeros(lift.shape, lift.dtype)
    lift[0:96, 0:48] = sum_mid.astype(jnp.bfloat16)
    lift[0:48, 64:128] = sum_coarse[:, 128:].astype(jnp.bfloat16)
    lift[96:144, :] = sum_coarse[:, :128].astype(jnp.bfloat16)

    edges = (
        dot(picks((32, 256), ((0, 0), (1, 1), (16, 254), (17, 255))), fine[...], 1, 1)
        + dot(picks((32, 256), ((2, 0), (18, 255))), in_fine[...], 1, 1)
        + dot(picks((32, 128), ((3, 0), (4, 1), (19, 126), (20, 127))), mid[...], 1, 1)
        + dot(picks((32, 128), ((5, 0), (21, 127))), in_mid[...], 1, 1)
    ).astype(jnp.bfloat16)
    masked = coarse[...].reshape(COARSE_ROWS * COARSE_COLS, COARSE)
    inner = inner_coarse[...].reshape(COARSE_ROWS * COARSE_COLS, COARSE)
    for side, out, cols in ((0, left, (0, 1, 0)), (1, right, (62, 63, 63))):
        for tile in range(12):
            out[tile * 16 : (tile + 1) * 16, :] = edges[side * 16 : (side + 1) * 16, tile * 128 : (tile + 1) * 128]
        row, cell = iota((32, 512), 0), iota((32, 512), 1)
        here = cell - (row % 8) * 64
        first = ((row < 8) & (here == cols[0])) | ((row >= 8) & (row < 16) & (here == cols[1]))
        second = (row >= 16) & (row < 24) & (here == cols[2])
        rim = dot(first.astype(jnp.float32).astype(jnp.bfloat16), masked) + dot(
            second.astype(jnp.float32).astype(jnp.bfloat16), inner
        )
        rim = rim.astype(jnp.bfloat16)
        out[192:224, :] = rim[:, :128]
        out[224:256, :] = jnp.zeros((32, 128), jnp.bfloat16)
        out[224:256, 0:64] = rim[:, 128:]

    for out, last in ((up, False), (down, True)):
        two = slice(CELLS - 2 * FINE, CELLS) if last else slice(0, 2 * FINE)
        one = slice(CELLS - FINE, CELLS) if last else slice(0, FINE)
        out[0:96, :] = fine[two, 0:128]
        out[96:192, :] = fine[two, 128:256]
        out[192:240, :] = in_fine[one, 0:128]
        out[240:288, :] = in_fine[one, 128:256]
        out[288:480, :] = mid[slice(CELLS - 2 * MID, CELLS) if last else slice(0, 2 * MID), :]
        out[480:576, :] = in_mid[slice(CELLS - MID, CELLS) if last else slice(0, MID), :]
        at = 6 if last else 0
        pair = coarse[at : at + 2].reshape(128, COARSE)
        out[576:704, :] = pair[:, :128]
        single = inner_coarse[7 if last else 0]
        out[704:768, :] = single[:, :128]
        out[768:896, :] = jnp.zeros((128, 128), jnp.bfloat16)
        out[768:896, 0:64] = pair[:, 128:]
        out[768:832, 64:128] = single[:, 128:]


def prep(*args):
    half = jnp.bfloat16
    shapes = (
        (CELLS, 256), (CELLS, 128), (COARSE_ROWS, COARSE_COLS, COARSE),
        (896, 128), (896, 128), (256, 128), (256, 128), (144, 128),
    )
    return pl.pallas_call(
        prep_kernel,
        out_shape=[jax.ShapeDtypeStruct(shape, half) for shape in shapes],
        scratch_shapes=[pltpu.VMEM((CELLS, width), half) for width in (256, 128, 256, 128)],
        compiler_params=PARAMS,
        name="prep",
    )(*args)


def unit_kernel(
    source, inner, masked, top, bottom, lt, rt, top_lt, top_rt, bottom_lt, bottom_rt, first, second,
    out, grads, mx, ix, px, sx, ox, acc_first, acc_second, *, chans, rows, width, edge, fill_rows, write_grads,
):
    ring = width + 128
    half = jnp.bfloat16

    mx[2 * chans : 2 * chans + CELLS, 0:width] = masked[...]
    ix[chans : chans + CELLS, 0:width] = jnp.transpose(inner[...], (1, 0, 2)).reshape(CELLS, width)
    sx[...] = jnp.transpose(source[...], (1, 0, 2)).reshape(CELLS, width)
    fill_rows(mx, ix, top, 0, 0)
    fill_rows(mx, ix, bottom, 2 * chans + CELLS, chans + CELLS)
    place = picks(
        (32, 256),
        ((edge, 0), (edge + 1, 1), (16 + edge, 126), (17 + edge, 127), (edge + 2, 128), (18 + edge, 255)),
    )

    def columns(right, left, tile):
        rows16 = slice(tile * 16, (tile + 1) * 16)
        both = jnp.concatenate([right[rows16, :], left[rows16, :]], axis=0)
        return dot(both, place, 0, 0).astype(half)

    for tile in range(12):
        cols = columns(rt, lt, tile)
        mx[2 * chans + tile * 128 : 2 * chans + (tile + 1) * 128, width:ring] = cols[:, :128]
        ix[chans + tile * 128 : chans + (tile + 1) * 128, width:ring] = cols[:, 128:]
    for tile in range((CELLS - 2 * chans) // 128, 12):
        cols = columns(top_rt, top_lt, tile)
        skip = max(0, CELLS - 2 * chans - tile * 128)
        at = tile * 128 + skip - (CELLS - 2 * chans)
        mx[at : at + 128 - skip, width:ring] = cols[skip:, :128]
        if tile == 11:
            ix[0:chans, width:ring] = cols[128 - chans :, 128:]
    for tile in range(-(-2 * chans // 128)):
        cols = columns(bottom_rt, bottom_lt, tile)
        size = min(128, 2 * chans - tile * 128)
        at = 2 * chans + CELLS + tile * 128
        mx[at : at + size, width:ring] = cols[:size, :128]
        if tile == 0:
            ix[chans + CELLS :, width:ring] = cols[:chans, 128:]

    def taps(weight, window):
        parts = dot(weight, window)
        return (
            pltpu.roll(parts[:chans], ring - 1, 1) + parts[chans : 2 * chans] + pltpu.roll(parts[2 * chans :], 1, 1)
        )

    def before(row, carry):
        at = pl.multiple_of(row * chans, 16)
        inner_grad = taps(second[...], mx[pl.ds(at, 3 * chans), :])
        px[pl.ds(at, chans), :] = keep(ix[pl.ds(at, chans), :].astype(jnp.float32), inner_grad).astype(half)
        return carry

    lax.fori_loop(0, rows + 2, before, 0, unroll=2)

    def spread(tile):
        wide = jnp.concatenate([tile.astype(jnp.float32), jnp.zeros((chans, 128), jnp.float32)], axis=1)
        return jnp.concatenate([pltpu.roll(wide, 1, 1), wide, pltpu.roll(wide, ring - 1, 1)], axis=0).astype(half)

    acc_first[...] = jnp.zeros(acc_first.shape, jnp.float32)
    acc_second[...] = jnp.zeros(acc_second.shape, jnp.float32)

    def after(row, carry):
        at = pl.multiple_of(row * chans, 16)
        window = px[pl.ds(at, 3 * chans), :]
        grad = taps(first[...], window)[:, :width]
        ox[pl.ds(row, 1), :, :] = (masked[pl.ds(at, chans), :].astype(jnp.float32) + grad).astype(half)[None]
        acc_first[...] += dot(spread(sx[pl.ds(at, chans), :]), window, 1, 1)
        own = ix[pl.ds(pl.multiple_of(at + chans, 16), chans), 0:width]
        acc_second[...] += dot(spread(own), mx[pl.ds(pl.multiple_of(at + chans, 16), 3 * chans), :], 1, 1)
        return carry

    lax.fori_loop(0, rows, after, 0, unroll=2)
    out[...] = jnp.transpose(ox[...], (1, 0, 2))
    write_grads(grads, acc_first, acc_second)


def fine_rows(mx, ix, halo, at, inner_at):
    mx[at : at + 96, 0:128] = halo[0:96, :]
    mx[at : at + 96, 128:256] = halo[96:192, :]
    ix[inner_at : inner_at + 48, 0:128] = halo[192:240, :]
    ix[inner_at : inner_at + 48, 128:256] = halo[240:288, :]


def mid_rows(mx, ix, halo, at, inner_at):
    mx[at : at + 192, 0:128] = halo[288:480, :]
    ix[inner_at : inner_at + 96, 0:128] = halo[480:576, :]


def fine_grads(grads, acc_first, acc_second):
    for tap in range(3):
        cols = slice((2 - tap) * FINE, (3 - tap) * FINE)
        pair = jnp.concatenate([acc_second[:, cols], acc_first[:, cols], jnp.zeros((144, 32), jnp.float32)], axis=1)
        grads[tap * 144 : (tap + 1) * 144, :] = pair.astype(jnp.bfloat16)


def mid_grads(grads, acc_first, acc_second):
    for index, acc in enumerate((acc_second, acc_first)):
        for tap in range(3):
            part = jnp.concatenate(
                [acc[:, (2 - tap) * MID : (3 - tap) * MID], jnp.zeros((288, 32), jnp.float32)], axis=1
            )
            at = (3 * index + tap) * 288
            grads[at : at + 288, :] = part.astype(jnp.bfloat16)


def channel_unit(source, inner, masked, halo, first, second, chans, rows, width, edge, fill_rows, grad_rows, write_grads, name):
    half = jnp.bfloat16
    ring = width + 128

    def kernel(*refs):
        unit_kernel(
            *refs, chans=chans, rows=rows, width=width, edge=edge, fill_rows=fill_rows, write_grads=write_grads
        )

    def stacked(weight):
        return jnp.transpose(weight[::-1], (1, 2, 0, 3)).reshape(3 * chans, 3 * chans)

    return pl.pallas_call(
        kernel,
        out_shape=[
            jax.ShapeDtypeStruct((chans, rows, width), half),
            jax.ShapeDtypeStruct((grad_rows, 128), half),
        ],
        scratch_shapes=[
            pltpu.VMEM(((rows + 4) * chans, ring), half),
            pltpu.VMEM(((rows + 2) * chans, ring), half),
            pltpu.VMEM(((rows + 2) * chans, ring), half),
            pltpu.VMEM((CELLS, width), half),
            pltpu.VMEM((rows, chans, width), half),
            pltpu.VMEM((3 * chans, 3 * chans), jnp.float32),
            pltpu.VMEM((3 * chans, 3 * chans), jnp.float32),
        ],
        compiler_params=PARAMS,
        name=name,
    )(source, inner, masked, *halo, stacked(first), stacked(second))


def coarse_places():
    place = np.zeros((2, 13 * 16, 6 * 32), np.float32)
    for index, first_row, count, sides in ((0, -2, 12, ((0, 0, "r"), (1, 1, "r"), (14, 0, "l"), (15, 1, "l"))), (1, -1, 10, ((0, 2, "r"), (15, 2, "l")))):
        for block in range(count + 1):
            for at, which, side in sides:
                row = first_row + block - (1 if side == "r" else 0)
                if row < first_row or row >= first_row + count:
                    continue
                message = 0 if 0 <= row < 8 else 1 if row < 0 else 2
                source = 2 * message + (0 if side == "r" else 1)
                place[index, block * 16 + at, source * 32 + which * 8 + row % 8] = 1
    return place.reshape(2 * 13 * 16, 6 * 32)


def coarse_kernel(
    source, inner, masked, top, bottom, lt, rt, top_lt, top_rt, bottom_lt, bottom_rt, first, second, place,
    out, grads, mx, ix, px, own, turned, tail,
):
    half = jnp.bfloat16
    lead = 16
    rims = jnp.concatenate(
        [
            jnp.concatenate([ref[192:224, :], ref[224:256, 0:64]], axis=1)
            for ref in (rt, lt, top_rt, top_lt, bottom_rt, bottom_lt)
        ],
        axis=0,
    )
    rims = dot(place[...], rims).astype(half)

    def rows_of(halo):
        pair = jnp.concatenate([halo[576:704, :], halo[768:896, 0:64]], axis=1)
        single = jnp.concatenate([halo[704:768, :], halo[768:832, 64:128]], axis=1)
        return pair, single

    above, above_inner = rows_of(top)
    below, below_inner = rows_of(bottom)
    grid = [above[:64], above[64:]] + [masked[k] for k in range(8)] + [below[:64], below[64:]]
    inner_grid = [above_inner] + [inner[k] for k in range(8)] + [below_inner]
    for ref, blocks, at in ((mx.at[1], grid, 0), (ix, inner_grid, 208)):
        ref[0:lead, :] = rims[at : at + 16]
        for k, block in enumerate(blocks):
            start = lead + k * PITCH
            ref[start : start + 64, :] = block
            ref[start + 64 : start + PITCH, :] = rims[at + (k + 1) * 16 : at + (k + 2) * 16]

    def shifted(ref, size):
        whole = ref[1].astype(jnp.float32)
        ref[0] = pltpu.roll(whole, size - 1, 0).astype(half)
        ref[2] = pltpu.roll(whole, 1, 0).astype(half)

    def taps(ref, weight, start, size):
        total = jnp.zeros((size, COARSE), jnp.float32)
        for row_tap in range(3):
            for col_tap in range(3):
                at = start + (2 - row_tap) * PITCH
                total += dot(ref[col_tap, at : at + size, :], weight[row_tap, col_tap], 1, 1)
        return total

    shifted(mx, 976)
    for start in range(0, 816, 272):
        inner_grad = taps(mx, second, start, 272)
        px[1, start : start + 272, :] = keep(
            ix[start : start + 272, :].astype(jnp.float32), inner_grad
        ).astype(half)
    shifted(px, 816)
    for row in range(8):
        grad = taps(px, first, lead + row * PITCH, 64)
        out[row] = (masked[row].astype(jnp.float32) + grad).astype(half)

    def corr(tile, ref, start, write):
        own[...] = jnp.zeros(own.shape, half)
        for row in range(8):
            own[row * PITCH : row * PITCH + 64, :] = tile[row]
        turned[...] = jnp.transpose(own[...].astype(jnp.float32)).astype(half)
        for row_tap in range(3):
            for col_tap in range(3):
                at = start + (2 - row_tap) * PITCH
                write(row_tap * 3 + col_tap, dot(turned[...], ref[col_tap, at : at + 8 * PITCH, :]))

    def write_second(tap, value):
        grads[tap * COARSE : (tap + 1) * COARSE, :] = value[:, :128].astype(half)
        tail[tap * COARSE : (tap + 1) * COARSE, :] = value[:, 128:].astype(half)

    def write_first(tap, value):
        at = 1728 + tap * COARSE
        grads[at : at + COARSE, :] = value[:, :128].astype(half)
        rows = slice(3456 + tap * COARSE, 3456 + (tap + 1) * COARSE)
        grads[rows, :] = jnp.concatenate(
            [tail[tap * COARSE : (tap + 1) * COARSE, :], value[:, 128:].astype(half)], axis=1
        )

    corr(inner, mx, lead + PITCH, write_second)
    corr(source, px, lead, write_first)
    grads[5184:, :] = jnp.zeros((192, 128), half)


def coarse_unit(source, inner, masked, halo, first, second):
    half = jnp.bfloat16
    return pl.pallas_call(
        coarse_kernel,
        out_shape=[
            jax.ShapeDtypeStruct((COARSE_ROWS, COARSE_COLS, COARSE), half),
            jax.ShapeDtypeStruct((5376, 128), half),
        ],
        scratch_shapes=[
            pltpu.VMEM((3, 976, COARSE), half),
            pltpu.VMEM((816, COARSE), half),
            pltpu.VMEM((3, 816, COARSE), half),
            pltpu.VMEM((8 * PITCH, COARSE), half),
            pltpu.VMEM((COARSE, 8 * PITCH), half),
            pltpu.VMEM((1728, 64), half),
        ],
        compiler_params=PARAMS,
        name="coarse_unit",
    )(source, inner, masked, *halo, first, second, jnp.asarray(coarse_places(), half))


def unpack_kernel(large, small, first_fine, second_fine, first_mid, second_mid, first_coarse, second_coarse, lift_mid, lift_coarse):
    full = jnp.float32
    for tap in range(9):
        row_tap, col_tap = tap // 3, tap % 3
        rows = slice(tap * COARSE, (tap + 1) * COARSE)
        tails = large[3456 + tap * COARSE : 3456 + (tap + 1) * COARSE, :].astype(full)
        second_coarse[row_tap, col_tap, :, 0:128] = large[rows, :].astype(full)
        second_coarse[row_tap, col_tap, :, 128:192] = tails[:, :64]
        first_coarse[row_tap, col_tap, :, 0:128] = large[1728 + tap * COARSE : 1728 + (tap + 1) * COARSE, :].astype(full)
        first_coarse[row_tap, col_tap, :, 128:192] = tails[:, 64:]
        pair = small[tap * FINE : (tap + 1) * FINE, :].astype(full)
        second_fine[row_tap, col_tap] = pair[:, 0:48]
        first_fine[row_tap, col_tap] = pair[:, 48:96]
        second_mid[row_tap, col_tap] = small[432 + tap * MID : 432 + (tap + 1) * MID, 0:96].astype(full)
        first_mid[row_tap, col_tap] = small[1296 + tap * MID : 1296 + (tap + 1) * MID, 0:96].astype(full)
    lift_mid[...] = small[2160:2256, 0:48].astype(full)
    wide = jnp.concatenate([small[2256:2304, :], small[2160:2208, 64:128]], axis=1).astype(full)
    lift_coarse[...] = jnp.transpose(wide)


def unpack(large, small):
    shapes = ((3, 3, 48, 48),) * 2 + ((3, 3, 96, 96),) * 2 + ((3, 3, 192, 192),) * 2 + ((96, 48), (192, 48))
    return pl.pallas_call(
        unpack_kernel,
        out_shape=[jax.ShapeDtypeStruct(shape, jnp.float32) for shape in shapes],
        compiler_params=PARAMS,
        name="unpack",
    )(large, small)


def on_device(
    grad_joined, joined_fine, input_fine, inner_fine, unit_fine, input_mid, inner_mid, unit_mid,
    input_coarse, inner_coarse, unit_coarse, first_fine, second_fine, first_mid, second_mid,
    first_coarse, second_coarse, lift_mid, lift_coarse,
):
    input_coarse, inner_coarse, unit_coarse = (
        jnp.transpose(x, (1, 2, 0)) for x in (input_coarse, inner_coarse, unit_coarse)
    )
    fine, mid, coarse, up, down, left, right, lift = prep(
        grad_joined, joined_fine, unit_fine, inner_fine, unit_mid, inner_mid, unit_coarse, inner_coarse, lift_mid, lift_coarse
    )
    halo = (
        send(down, shift_pairs(1, 0)),
        send(up, shift_pairs(-1, 0)),
        send(right, shift_pairs(0, 1)),
        send(left, shift_pairs(0, -1)),
        send(right, shift_pairs(1, 1)),
        send(left, shift_pairs(1, -1)),
        send(right, shift_pairs(-1, 1)),
        send(left, shift_pairs(-1, -1)),
    )
    coarse_input, large = coarse_unit(input_coarse, inner_coarse, coarse, halo, first_coarse, second_coarse)
    mid_input, mid_part = channel_unit(
        input_mid, inner_mid, mid, halo, first_mid, second_mid, MID, 16, 128, 3, mid_rows, 1728, mid_grads, "mid_unit"
    )
    fine_input, fine_part = channel_unit(
        input_fine, inner_fine, fine, halo, first_fine, second_fine, FINE, 32, 256, 0, fine_rows, 432, fine_grads, "fine_unit"
    )
    large = all_sum(large)
    small = all_sum(jnp.concatenate([fine_part, mid_part, lift]))
    grads = unpack(large, small)
    return (fine_input, mid_input, jnp.transpose(coarse_input, (2, 0, 1)), *grads)


def solution(mesh):
    tiled = P(None, "row", "col")
    return jax.shard_map(
        on_device,
        mesh=mesh,
        in_specs=(tiled,) * 11 + (P(),) * 8,
        out_specs=(tiled,) * 3 + (P(),) * 8,
        check_vma=False,
    )
```

```python
import jax
import jax.numpy as jnp
import numpy as np
from jax import lax
from jax.experimental import pallas as pl
from jax.experimental.pallas import tpu as pltpu
from jax.sharding import PartitionSpec as P

ROWS, COLS = 32, 4
CELLS = 1536
FINE, MID = 48, 96
COARSE_ROWS, COARSE_COLS, COARSE = 8, 64, 192
PITCH = 80
PARAMS = pltpu.CompilerParams(vmem_limit_bytes=56 * 2**20)

AXES = ("row", "col")
ORDER = (("y", "x", "z"), ("x", "z", "y"))
CORE_PAIRS = [(d, d ^ 4) for d in range(128)]


def stage_pairs(stage, k):
    pairs = []
    for d in range(128):
        row, col = divmod(d, 4)
        at = {"x": row // 8, "z": (row // 2) % 4, "y": col}
        core = row % 2
        at[ORDER[core][stage]] ^= k
        pairs.append((d, (at["x"] * 8 + at["z"] * 2 + core) * 4 + at["y"]))
    return pairs


def my_place():
    row, col = lax.axis_index("row"), lax.axis_index("col")
    at = {"x": row // 8, "z": (row // 2) % 4, "y": col}
    core = row % 2
    return core, [jnp.where(core == 0, at[ORDER[0][s]], at[ORDER[1][s]]) for s in range(3)]


def send(block, pairs):
    return lax.ppermute(block, AXES, pairs)


def add4(own, others):
    a, b, c = [other.astype(jnp.float32) for other in others]
    return ((own.astype(jnp.float32) + a) + (b + c)).astype(jnp.bfloat16)


def scatter_stage(block, stage, mine):
    parts = block.reshape(4, block.shape[0] // 4, block.shape[1])
    own = lax.dynamic_index_in_dim(parts, mine, 0, keepdims=False)
    others = [
        send(lax.dynamic_index_in_dim(parts, mine ^ k, 0, keepdims=False), stage_pairs(stage, k))
        for k in (1, 2, 3)
    ]
    return add4(own, others)


def reduce_stage(block, stage):
    return add4(block, [send(block, stage_pairs(stage, k)) for k in (1, 2, 3)])


def gather_stage(block, stage, mine):
    parts = [block] + [send(block, stage_pairs(stage, k)) for k in (1, 2, 3)]
    whole = jnp.zeros((4,) + block.shape, block.dtype)
    for k in range(4):
        whole = lax.dynamic_update_index_in_dim(whole, parts[k], mine ^ k, 0)
    return whole.reshape(4 * block.shape[0], block.shape[1])


def beside(stage, block, work, *operands):
    block, *operands = lax.optimization_barrier((block, *operands))
    return lax.optimization_barrier((stage(block), work(*operands)))


def all_sum(block, works):
    core, mine = my_place()
    half = block.shape[0] // 2
    halves = block.reshape(2, half, block.shape[1])
    other = send(lax.dynamic_index_in_dim(halves, 1 - core, 0, keepdims=False), CORE_PAIRS)
    own = lax.dynamic_index_in_dim(halves, core, 0, keepdims=False)
    part = (own.astype(jnp.float32) + other.astype(jnp.float32)).astype(jnp.bfloat16)
    part, out_0 = beside(lambda x: scatter_stage(x, 0, mine[0]), part, *works[0])
    part = scatter_stage(part, 1, mine[1])
    part = reduce_stage(part, 2)
    part, out_1 = beside(lambda x: gather_stage(x, 1, mine[1]), part, *works[1])
    part, out_2 = beside(lambda x: gather_stage(x, 0, mine[0]), part, *works[2])
    other = send(part, CORE_PAIRS)
    whole = jnp.where(core == 0, jnp.concatenate([part, other]), jnp.concatenate([other, part]))
    return whole, out_0, out_1, out_2


def partner(at, count, pairing):
    other = at + 1 if at % 2 == pairing else at - 1
    return other if 0 <= other < count else None


def swap_pairs(row_pairing, col_pairing):
    pairs = []
    for row in range(ROWS):
        for col in range(COLS):
            to_row = row if row_pairing is None else partner(row, ROWS, row_pairing)
            to_col = col if col_pairing is None else partner(col, COLS, col_pairing)
            if to_row is not None and to_col is not None:
                pairs.append((row * COLS + col, to_row * COLS + to_col))
    return pairs


def iota(shape, dim):
    return lax.broadcasted_iota(jnp.int32, shape, dim)


def picks(shape, pairs):
    rows, cols = iota(shape, 0), iota(shape, 1)
    hit = jnp.zeros(shape, jnp.bool_)
    for row, col in pairs:
        hit = hit | ((rows == row) & (cols == col))
    return hit.astype(jnp.float32).astype(jnp.bfloat16)


def dot(a, b, a_dim=1, b_dim=0):
    return lax.dot_general(
        a, b, (((a_dim,), (b_dim,)), ((), ())), preferred_element_type=jnp.float32
    )


def keep(gate, value):
    return jnp.where(gate > 0, value, jnp.zeros_like(value))


def prep_kernel(
    parity, grad, joined, unit_fine, inner_fine, unit_mid, inner_mid, unit_coarse, inner_coarse, lift_mid, lift_coarse,
    fine, mid, coarse, row_0, row_1, col_0, col_1, lift, upstream, gate_mid, in_fine, in_mid,
):
    above = keep(joined[...], grad[...])
    upstream[...] = jnp.transpose(above, (1, 0, 2)).reshape(CELLS, 256)
    fine[...] = jnp.transpose(keep(unit_fine[...], above), (1, 0, 2)).reshape(CELLS, 256)
    gate_mid[...] = jnp.transpose(unit_mid[...], (1, 0, 2)).reshape(CELLS, 128)
    in_fine[...] = jnp.transpose(inner_fine[...], (1, 0, 2)).reshape(CELLS, 256)
    in_mid[...] = jnp.transpose(inner_mid[...], (1, 0, 2)).reshape(CELLS, 128)

    cells, target = iota((256, 192), 0), iota((256, 192), 1)
    pooling = jnp.where(target < 128, cells // 2, cells // 4 + 128) == target
    pooling = pooling.astype(jnp.float32).astype(jnp.bfloat16)
    sum_mid = jnp.zeros((FINE, MID), jnp.float32)
    sum_coarse = jnp.zeros((FINE, COARSE), jnp.float32)
    for row in range(COARSE_ROWS):
        pooled = dot(upstream[row * 192 : (row + 1) * 192, :], pooling)
        quarter = [pooled[k * FINE : (k + 1) * FINE] for k in range(4)]
        for half in range(2):
            cell = (quarter[2 * half] + quarter[2 * half + 1])[:, :128].astype(jnp.bfloat16)
            rows = slice((2 * row + half) * MID, (2 * row + half + 1) * MID)
            gate = gate_mid[rows, :]
            mid[rows, :] = keep(gate, dot(lift_mid[...], cell, 0, 0).astype(jnp.bfloat16))
            sum_mid += dot(cell, gate, 1, 1)
        cell = ((quarter[0] + quarter[1]) + (quarter[2] + quarter[3]))[:, 128:].astype(jnp.bfloat16)
        gate = unit_coarse[row]
        coarse[row] = keep(gate, dot(cell, lift_coarse[...], 0, 0).astype(jnp.bfloat16))
        sum_coarse += dot(cell, gate)

    lift[...] = jnp.zeros(lift.shape, lift.dtype)
    lift[0:48, 0:96] = sum_mid.astype(jnp.bfloat16)
    lift[48:96, 0:64] = sum_coarse[:, 128:].astype(jnp.bfloat16)
    lift[96:144, :] = sum_coarse[:, :128].astype(jnp.bfloat16)

    edges = (
        dot(picks((32, 256), ((0, 0), (1, 1), (16, 254), (17, 255))), fine[...], 1, 1)
        + dot(picks((32, 256), ((2, 0), (18, 255))), in_fine[...], 1, 1)
        + dot(picks((32, 128), ((3, 0), (4, 1), (19, 126), (20, 127))), mid[...], 1, 1)
        + dot(picks((32, 128), ((5, 0), (21, 127))), in_mid[...], 1, 1)
    ).astype(jnp.bfloat16)
    masked = coarse[...].reshape(COARSE_ROWS * COARSE_COLS, COARSE)
    inner = inner_coarse[...].reshape(COARSE_ROWS * COARSE_COLS, COARSE)
    sides = []
    for side, cols in ((0, (0, 1, 0)), (1, (62, 63, 63))):
        row, cell = iota((32, 512), 0), iota((32, 512), 1)
        here = cell - (row % 8) * 64
        first = ((row < 8) & (here == cols[0])) | ((row >= 8) & (row < 16) & (here == cols[1]))
        second = (row >= 16) & (row < 24) & (here == cols[2])
        rim = dot(first.astype(jnp.float32).astype(jnp.bfloat16), masked) + dot(
            second.astype(jnp.float32).astype(jnp.bfloat16), inner
        )
        sides.append((edges[side * 16 : (side + 1) * 16], rim.astype(jnp.bfloat16)))
    for out, to_right in ((col_0, parity[1] == 0), (col_1, parity[1] == 1)):
        edge = jnp.where(to_right, sides[1][0], sides[0][0])
        rim = jnp.where(to_right, sides[1][1], sides[0][1])
        for tile in range(12):
            out[tile * 16 : (tile + 1) * 16, :] = edge[:, tile * 128 : (tile + 1) * 128]
        out[192:224, :] = rim[:, :128]
        out[224:256, :] = jnp.zeros((32, 128), jnp.bfloat16)
        out[224:256, 0:64] = rim[:, 128:]

    for out, last in ((row_0, parity[0] == 0), (row_1, parity[0] == 1)):

        def rim_rows(size):
            return pl.ds(pl.multiple_of(jnp.where(last, CELLS - size, 0), 16), size)

        out[0:96, :] = fine[rim_rows(2 * FINE), 0:128]
        out[96:192, :] = fine[rim_rows(2 * FINE), 128:256]
        out[192:240, :] = in_fine[rim_rows(FINE), 0:128]
        out[240:288, :] = in_fine[rim_rows(FINE), 128:256]
        out[288:480, :] = mid[rim_rows(2 * MID), :]
        out[480:576, :] = in_mid[rim_rows(MID), :]
        pair = coarse[pl.ds(jnp.where(last, 6, 0), 2)].reshape(128, COARSE)
        out[576:704, :] = pair[:, :128]
        single = inner_coarse[pl.ds(jnp.where(last, 7, 0), 1)].reshape(64, COARSE)
        out[704:768, :] = single[:, :128]
        out[768:896, :] = jnp.zeros((128, 128), jnp.bfloat16)
        out[768:896, 0:64] = pair[:, 128:]
        out[768:832, 64:128] = single[:, 128:]


IN_SMEM = pl.BlockSpec(memory_space=pltpu.SMEM)
IN_VMEM = pl.BlockSpec(memory_space=pltpu.VMEM)


class Halo:
    def __init__(self, parity, refs):
        row_0, row_1, col_0, col_1, *corner = [ref[...] for ref in refs]
        row_even, col_even = parity[0] == 0, parity[1] == 0
        self.top, self.bottom = jnp.where(row_even, row_1, row_0), jnp.where(row_even, row_0, row_1)
        self.left, self.right = jnp.where(col_even, col_1, col_0), jnp.where(col_even, col_0, col_1)
        left = [jnp.where(col_even, corner[2 * p + 1], corner[2 * p]) for p in range(2)]
        right = [jnp.where(col_even, corner[2 * p], corner[2 * p + 1]) for p in range(2)]
        self.top_left, self.bottom_left = jnp.where(row_even, left[1], left[0]), jnp.where(row_even, left[0], left[1])
        self.top_right, self.bottom_right = jnp.where(row_even, right[1], right[0]), jnp.where(row_even, right[0], right[1])


def prep(*args):
    half = jnp.bfloat16
    shapes = (
        (CELLS, 256), (CELLS, 128), (COARSE_ROWS, COARSE_COLS, COARSE),
        (896, 128), (896, 128), (256, 128), (256, 128), (144, 128),
    )
    return pl.pallas_call(
        prep_kernel,
        out_shape=[jax.ShapeDtypeStruct(shape, half) for shape in shapes],
        in_specs=[IN_SMEM] + [IN_VMEM] * 10,
        scratch_shapes=[pltpu.VMEM((CELLS, width), half) for width in (256, 128, 256, 128)],
        compiler_params=PARAMS,
        name="prep",
    )(*args)


def unit_kernel(
    parity, *refs, chans, rows, width, edge, fill_rows, write_grads,
):
    halo = Halo(parity, refs[:8])
    source, inner, masked, second, px, grads, mx, ix, sx, acc_first, acc_second = refs[8:]
    ring = width + 128
    half = jnp.bfloat16

    mx[2 * chans : 2 * chans + CELLS, 0:width] = masked[...]
    ix[chans : chans + CELLS, 0:width] = jnp.transpose(inner[...], (1, 0, 2)).reshape(CELLS, width)
    sx[...] = jnp.transpose(source[...], (1, 0, 2)).reshape(CELLS, width)
    fill_rows(mx, ix, halo.top, 0, 0)
    fill_rows(mx, ix, halo.bottom, 2 * chans + CELLS, chans + CELLS)
    place = picks(
        (32, 256),
        ((edge, 0), (edge + 1, 1), (16 + edge, 126), (17 + edge, 127), (edge + 2, 128), (18 + edge, 255)),
    )

    def columns(right, left, tile):
        rows16 = slice(tile * 16, (tile + 1) * 16)
        both = jnp.concatenate([right[rows16, :], left[rows16, :]], axis=0)
        return dot(both, place, 0, 0).astype(half)

    for tile in range(12):
        cols = columns(halo.right, halo.left, tile)
        mx[2 * chans + tile * 128 : 2 * chans + (tile + 1) * 128, width:ring] = cols[:, :128]
        ix[chans + tile * 128 : chans + (tile + 1) * 128, width:ring] = cols[:, 128:]
    for tile in range((CELLS - 2 * chans) // 128, 12):
        cols = columns(halo.top_right, halo.top_left, tile)
        skip = max(0, CELLS - 2 * chans - tile * 128)
        at = tile * 128 + skip - (CELLS - 2 * chans)
        mx[at : at + 128 - skip, width:ring] = cols[skip:, :128]
        if tile == 11:
            ix[0:chans, width:ring] = cols[128 - chans :, 128:]
    for tile in range(-(-2 * chans // 128)):
        cols = columns(halo.bottom_right, halo.bottom_left, tile)
        size = min(128, 2 * chans - tile * 128)
        at = 2 * chans + CELLS + tile * 128
        mx[at : at + size, width:ring] = cols[:size, :128]
        if tile == 0:
            ix[chans + CELLS :, width:ring] = cols[:chans, 128:]

    def before(row, carry):
        at = pl.multiple_of(row * chans, 16)
        inner_grad = ring_taps(second[...], mx[pl.ds(at, 3 * chans), :], chans, ring)
        px[pl.ds(at, chans), :] = keep(ix[pl.ds(at, chans), :].astype(jnp.float32), inner_grad).astype(half)
        return carry

    lax.fori_loop(0, rows + 2, before, 0, unroll=2)

    def spread(tile):
        wide = jnp.concatenate([tile.astype(jnp.float32), jnp.zeros((chans, 128), jnp.float32)], axis=1)
        return jnp.concatenate([pltpu.roll(wide, 1, 1), wide, pltpu.roll(wide, ring - 1, 1)], axis=0).astype(half)

    acc_first[...] = jnp.zeros(acc_first.shape, jnp.float32)
    acc_second[...] = jnp.zeros(acc_second.shape, jnp.float32)

    def after(row, carry):
        at = pl.multiple_of(row * chans, 16)
        window = px[pl.ds(at, 3 * chans), :]
        acc_first[...] += dot(spread(sx[pl.ds(at, chans), :]), window, 1, 1)
        own = ix[pl.ds(pl.multiple_of(at + chans, 16), chans), 0:width]
        acc_second[...] += dot(spread(own), mx[pl.ds(pl.multiple_of(at + chans, 16), 3 * chans), :], 1, 1)
        return carry

    lax.fori_loop(0, rows, after, 0, unroll=2)
    write_grads(grads, acc_first, acc_second)


def ring_taps(weight, window, chans, ring):
    parts = dot(weight, window)
    return pltpu.roll(parts[:chans], ring - 1, 1) + parts[chans : 2 * chans] + pltpu.roll(parts[2 * chans :], 1, 1)


def input_kernel(masked, px, first, out, ox, *, chans, rows, width):
    def step(row, carry):
        at = pl.multiple_of(row * chans, 16)
        grad = ring_taps(first[...], px[pl.ds(at, 3 * chans), :], chans, width + 128)[:, :width]
        ox[pl.ds(row, 1), :, :] = (masked[pl.ds(at, chans), :].astype(jnp.float32) + grad).astype(jnp.bfloat16)[None]
        return carry

    lax.fori_loop(0, rows, step, 0, unroll=2)
    out[...] = jnp.transpose(ox[...], (1, 0, 2))


def fine_rows(mx, ix, halo, at, inner_at):
    mx[at : at + 96, 0:128] = halo[0:96, :]
    mx[at : at + 96, 128:256] = halo[96:192, :]
    ix[inner_at : inner_at + 48, 0:128] = halo[192:240, :]
    ix[inner_at : inner_at + 48, 128:256] = halo[240:288, :]


def mid_rows(mx, ix, halo, at, inner_at):
    mx[at : at + 192, 0:128] = halo[288:480, :]
    ix[inner_at : inner_at + 96, 0:128] = halo[480:576, :]


def fine_grads(grads, acc_first, acc_second):
    for tap in range(3):
        cols = slice((2 - tap) * FINE, (3 - tap) * FINE)
        pair = jnp.concatenate([acc_second[:, cols], acc_first[:, cols], jnp.zeros((144, 32), jnp.float32)], axis=1)
        grads[tap * 144 : (tap + 1) * 144, :] = pair.astype(jnp.bfloat16)


def mid_grads(grads, acc_first, acc_second):
    for index, acc in enumerate((acc_second, acc_first)):
        for tap in range(3):
            part = jnp.concatenate(
                [acc[:, (2 - tap) * MID : (3 - tap) * MID], jnp.zeros((288, 32), jnp.float32)], axis=1
            )
            at = (3 * index + tap) * 288
            grads[at : at + 288, :] = part.astype(jnp.bfloat16)


def channel_grads(parity, halo, source, inner, masked, second, chans, rows, width, edge, fill_rows, grad_rows, write_grads, name):
    half = jnp.bfloat16
    ring = width + 128

    def kernel(*refs):
        unit_kernel(
            *refs, chans=chans, rows=rows, width=width, edge=edge, fill_rows=fill_rows, write_grads=write_grads
        )

    return pl.pallas_call(
        kernel,
        out_shape=[
            jax.ShapeDtypeStruct(((rows + 2) * chans, ring), half),
            jax.ShapeDtypeStruct((grad_rows, 128), half),
        ],
        in_specs=[IN_SMEM] + [IN_VMEM] * 12,
        scratch_shapes=[
            pltpu.VMEM(((rows + 4) * chans, ring), half),
            pltpu.VMEM(((rows + 2) * chans, ring), half),
            pltpu.VMEM((CELLS, width), half),
            pltpu.VMEM((3 * chans, 3 * chans), jnp.float32),
            pltpu.VMEM((3 * chans, 3 * chans), jnp.float32),
        ],
        compiler_params=PARAMS,
        name=name,
    )(parity, *halo, source, inner, masked, stacked(second, chans))


def stacked(weight, chans):
    return jnp.transpose(weight[::-1], (1, 2, 0, 3)).reshape(3 * chans, 3 * chans)


def channel_input(masked, px, first, chans, rows, width, name):
    def kernel(*refs):
        input_kernel(*refs, chans=chans, rows=rows, width=width)

    return pl.pallas_call(
        kernel,
        out_shape=jax.ShapeDtypeStruct((chans, rows, width), jnp.bfloat16),
        scratch_shapes=[pltpu.VMEM((rows, chans, width), jnp.bfloat16)],
        compiler_params=PARAMS,
        name=name,
    )(masked, px, stacked(first, chans))


def coarse_places():
    place = np.zeros((2, 13 * 16, 6 * 32), np.float32)
    for index, first_row, count, sides in ((0, -2, 12, ((0, 0, "r"), (1, 1, "r"), (14, 0, "l"), (15, 1, "l"))), (1, -1, 10, ((0, 2, "r"), (15, 2, "l")))):
        for block in range(count + 1):
            for at, which, side in sides:
                row = first_row + block - (1 if side == "r" else 0)
                if row < first_row or row >= first_row + count:
                    continue
                message = 0 if 0 <= row < 8 else 1 if row < 0 else 2
                source = 2 * message + (0 if side == "r" else 1)
                place[index, block * 16 + at, source * 32 + which * 8 + row % 8] = 1
    return place.reshape(2 * 13 * 16, 6 * 32)


def coarse_taps(ref, weight, start, size):
    total = jnp.zeros((size, COARSE), jnp.float32)
    for row_tap in range(3):
        for col_tap in range(3):
            at = start + (2 - row_tap) * PITCH
            total += dot(ref[col_tap, at : at + size, :], weight[row_tap, col_tap], 1, 1)
    return total


def coarse_kernel(parity, *refs):
    halo = Halo(parity, refs[:8])
    source, inner, masked, second, place, px, grads, mx, ix, own, turned, tail = refs[8:]
    half = jnp.bfloat16
    lead = 16
    rims = jnp.concatenate(
        [
            jnp.concatenate([ref[192:224, :], ref[224:256, 0:64]], axis=1)
            for ref in (halo.right, halo.left, halo.top_right, halo.top_left, halo.bottom_right, halo.bottom_left)
        ],
        axis=0,
    )
    rims = dot(place[...], rims).astype(half)

    def rows_of(rim):
        pair = jnp.concatenate([rim[576:704, :], rim[768:896, 0:64]], axis=1)
        single = jnp.concatenate([rim[704:768, :], rim[768:832, 64:128]], axis=1)
        return pair, single

    above, above_inner = rows_of(halo.top)
    below, below_inner = rows_of(halo.bottom)
    grid = [above[:64], above[64:]] + [masked[k] for k in range(8)] + [below[:64], below[64:]]
    inner_grid = [above_inner] + [inner[k] for k in range(8)] + [below_inner]
    for ref, blocks, at in ((mx.at[1], grid, 0), (ix, inner_grid, 208)):
        ref[0:lead, :] = rims[at : at + 16]
        for k, block in enumerate(blocks):
            start = lead + k * PITCH
            ref[start : start + 64, :] = block
            ref[start + 64 : start + PITCH, :] = rims[at + (k + 1) * 16 : at + (k + 2) * 16]

    def shifted(ref, size):
        whole = ref[1].astype(jnp.float32)
        ref[0] = pltpu.roll(whole, size - 1, 0).astype(half)
        ref[2] = pltpu.roll(whole, 1, 0).astype(half)

    shifted(mx, 976)
    for start in range(0, 816, 272):
        inner_grad = coarse_taps(mx, second, start, 272)
        px[1, start : start + 272, :] = keep(
            ix[start : start + 272, :].astype(jnp.float32), inner_grad
        ).astype(half)
    shifted(px, 816)
    def corr(tile, ref, start, write):
        own[...] = jnp.zeros(own.shape, half)
        for row in range(8):
            own[row * PITCH : row * PITCH + 64, :] = tile[row]
        turned[...] = jnp.transpose(own[...].astype(jnp.float32)).astype(half)
        for row_tap in range(3):
            for col_tap in range(3):
                at = start + (2 - row_tap) * PITCH
                write(row_tap * 3 + col_tap, dot(turned[...], ref[col_tap, at : at + 8 * PITCH, :]))

    def write_second(tap, value):
        grads[tap * COARSE : (tap + 1) * COARSE, :] = value[:, :128].astype(half)
        tail[tap * COARSE : (tap + 1) * COARSE, :] = value[:, 128:].astype(half)

    def write_first(tap, value):
        at = 1728 + tap * COARSE
        grads[at : at + COARSE, :] = value[:, :128].astype(half)
        rows = slice(3456 + tap * COARSE, 3456 + (tap + 1) * COARSE)
        grads[rows, :] = jnp.concatenate(
            [tail[tap * COARSE : (tap + 1) * COARSE, :], value[:, 128:].astype(half)], axis=1
        )

    corr(inner, mx, lead + PITCH, write_second)
    corr(source, px, lead, write_first)


def coarse_grads(parity, halo, source, inner, masked, second):
    half = jnp.bfloat16
    return pl.pallas_call(
        coarse_kernel,
        out_shape=[
            jax.ShapeDtypeStruct((3, 816, COARSE), half),
            jax.ShapeDtypeStruct((5184, 128), half),
        ],
        in_specs=[IN_SMEM] + [IN_VMEM] * 13,
        scratch_shapes=[
            pltpu.VMEM((3, 976, COARSE), half),
            pltpu.VMEM((816, COARSE), half),
            pltpu.VMEM((8 * PITCH, COARSE), half),
            pltpu.VMEM((COARSE, 8 * PITCH), half),
            pltpu.VMEM((1728, 64), half),
        ],
        compiler_params=PARAMS,
        name="coarse_grads",
    )(parity, *halo, source, inner, masked, second, jnp.asarray(coarse_places(), half))


def coarse_input_kernel(masked, px, first, out):
    for row in range(8):
        grad = coarse_taps(px, first, 16 + row * PITCH, 64)
        out[row] = (masked[row].astype(jnp.float32) + grad).astype(jnp.bfloat16)


def coarse_input(masked, px, first):
    return pl.pallas_call(
        coarse_input_kernel,
        out_shape=jax.ShapeDtypeStruct((COARSE_ROWS, COARSE_COLS, COARSE), jnp.bfloat16),
        compiler_params=PARAMS,
        name="coarse_input",
    )(masked, px, first)


AT_MID, AT_FINE, AT_LIFT, SUM_ROWS = 5184, 6912, 7344, 7680


def unpack_kernel(summed, first_fine, second_fine, first_mid, second_mid, first_coarse, second_coarse, lift_mid, lift_coarse):
    def part(start, size, lanes=slice(0, 128)):
        return summed[start : start + size, lanes].astype(jnp.float32)

    for tap in range(9):
        row_tap, col_tap = tap // 3, tap % 3
        tails = part(3456 + tap * COARSE, COARSE)
        second_coarse[row_tap, col_tap, :, 0:128] = part(tap * COARSE, COARSE)
        second_coarse[row_tap, col_tap, :, 128:192] = tails[:, :64]
        first_coarse[row_tap, col_tap, :, 0:128] = part(1728 + tap * COARSE, COARSE)
        first_coarse[row_tap, col_tap, :, 128:192] = tails[:, 64:]
        pair = part(AT_FINE + tap * FINE, FINE)
        second_fine[row_tap, col_tap] = pair[:, 0:48]
        first_fine[row_tap, col_tap] = pair[:, 48:96]
        second_mid[row_tap, col_tap] = part(AT_MID + tap * MID, MID, slice(0, 96))
        first_mid[row_tap, col_tap] = part(AT_MID + 864 + tap * MID, MID, slice(0, 96))
    lift_mid[...] = part(AT_LIFT, 48, slice(0, 96))
    lift_coarse[:, 0:128] = part(AT_LIFT + 96, 48)
    lift_coarse[:, 128:192] = part(AT_LIFT + 48, 48, slice(0, 64))


def unpack(summed):
    shapes = ((3, 3, 48, 48),) * 2 + ((3, 3, 96, 96),) * 2 + ((3, 3, 192, 192),) * 2 + ((48, 96), (48, 192))
    *taps, lift_mid, lift_coarse = pl.pallas_call(
        unpack_kernel,
        out_shape=[jax.ShapeDtypeStruct(shape, jnp.float32) for shape in shapes],
        compiler_params=PARAMS,
        name="unpack",
    )(summed)
    return *taps, jnp.transpose(lift_mid), jnp.transpose(lift_coarse)


def on_device(
    grad_joined, joined_fine, input_fine, inner_fine, unit_fine, input_mid, inner_mid, unit_mid,
    input_coarse, inner_coarse, unit_coarse, first_fine, second_fine, first_mid, second_mid,
    first_coarse, second_coarse, lift_mid, lift_coarse,
):
    input_coarse, inner_coarse, unit_coarse = (
        jnp.transpose(x, (1, 2, 0)) for x in (input_coarse, inner_coarse, unit_coarse)
    )
    parity = jnp.stack([lax.axis_index("row") % 2, lax.axis_index("col") % 2]).astype(jnp.int32)
    fine, mid, coarse, row_0, row_1, col_0, col_1, lift = prep(
        parity, grad_joined, joined_fine, unit_fine, inner_fine, unit_mid, inner_mid, unit_coarse, inner_coarse,
        jnp.transpose(lift_mid), jnp.transpose(lift_coarse),
    )
    halo = (
        send(row_0, swap_pairs(0, None)),
        send(row_1, swap_pairs(1, None)),
        send(col_0, swap_pairs(None, 0)),
        send(col_1, swap_pairs(None, 1)),
        send(col_0, swap_pairs(0, 0)),
        send(col_1, swap_pairs(0, 1)),
        send(col_0, swap_pairs(1, 0)),
        send(col_1, swap_pairs(1, 1)),
    )
    coarse_px, coarse_part = coarse_grads(parity, halo, input_coarse, inner_coarse, coarse, second_coarse)
    mid_px, mid_part = channel_grads(
        parity, halo, input_mid, inner_mid, mid, second_mid, MID, 16, 128, 3, mid_rows, 1728, mid_grads, "mid_grads"
    )
    fine_px, fine_part = channel_grads(
        parity, halo, input_fine, inner_fine, fine, second_fine, FINE, 32, 256, 0, fine_rows, 432, fine_grads, "fine_grads"
    )
    unused = jnp.zeros((SUM_ROWS - AT_LIFT - 144, 128), jnp.bfloat16)
    summed, fine_input, mid_input, input_grad = all_sum(
        jnp.concatenate([coarse_part, mid_part, fine_part, lift, unused]),
        (
            (lambda px: channel_input(fine, px, first_fine, FINE, 32, 256, "fine_input"), fine_px),
            (lambda px: channel_input(mid, px, first_mid, MID, 16, 128, "mid_input"), mid_px),
            (lambda px: coarse_input(coarse, px, first_coarse), coarse_px),
        ),
    )
    return (fine_input, mid_input, jnp.transpose(input_grad, (2, 0, 1)), *unpack(summed))


def solution(mesh):
    tiled = P(None, "row", "col")
    return jax.shard_map(
        on_device,
        mesh=mesh,
        in_specs=(tiled,) * 11 + (P(),) * 8,
        out_specs=(tiled,) * 3 + (P(),) * 8,
        check_vma=False,
    )
```

```python
import jax
import jax.numpy as jnp
import numpy as np
from jax import lax
from jax.experimental import pallas as pl
from jax.experimental.pallas import tpu as pltpu
from jax.sharding import PartitionSpec as P

ROWS, COLS = 32, 4
CELLS = 1536
FINE, MID = 48, 96
COARSE_ROWS, COARSE_COLS, COARSE = 8, 64, 192
PITCH = 80
AT_MID, AT_FINE, AT_LIFT, SUM_ROWS = 5184, 6912, 7344, 7680
PARAMS = pltpu.CompilerParams(vmem_limit_bytes=56 * 2**20)

AXES = ("row", "col")
ORDER = (("y", "x", "z"), ("x", "z", "y"))
CORE_PAIRS = [(d, d ^ 4) for d in range(128)]


def stage_pairs(stage, k):
    pairs = []
    for d in range(128):
        row, col = divmod(d, 4)
        at = {"x": row // 8, "z": (row // 2) % 4, "y": col}
        core = row % 2
        at[ORDER[core][stage]] ^= k
        pairs.append((d, (at["x"] * 8 + at["z"] * 2 + core) * 4 + at["y"]))
    return pairs


def my_place():
    row, col = lax.axis_index("row"), lax.axis_index("col")
    at = {"x": row // 8, "z": (row // 2) % 4, "y": col}
    core = row % 2
    return core, [jnp.where(core == 0, at[ORDER[0][s]], at[ORDER[1][s]]) for s in range(3)]


def send(block, pairs):
    return lax.ppermute(block, AXES, pairs)


def add4(own, others):
    a, b, c = [other.astype(jnp.float32) for other in others]
    return ((own.astype(jnp.float32) + a) + (b + c)).astype(jnp.bfloat16)


def scatter_stage(block, stage, mine):
    parts = block.reshape(4, block.shape[0] // 4, block.shape[1])
    own = lax.dynamic_index_in_dim(parts, mine, 0, keepdims=False)
    others = [
        send(lax.dynamic_index_in_dim(parts, mine ^ k, 0, keepdims=False), stage_pairs(stage, k))
        for k in (1, 2, 3)
    ]
    return add4(own, others)


def reduce_stage(block, stage):
    return add4(block, [send(block, stage_pairs(stage, k)) for k in (1, 2, 3)])


def gather_stage(block, stage, mine):
    parts = [block] + [send(block, stage_pairs(stage, k)) for k in (1, 2, 3)]
    whole = jnp.zeros((4,) + block.shape, block.dtype)
    for k in range(4):
        whole = lax.dynamic_update_index_in_dim(whole, parts[k], mine ^ k, 0)
    return whole.reshape(4 * block.shape[0], block.shape[1])


def beside(stage, block, work, *operands):
    block, *operands = lax.optimization_barrier((block, *operands))
    return lax.optimization_barrier((stage(block), work(*operands)))


def all_sum(kept, given, works):
    _, mine = my_place()
    part = (kept.astype(jnp.float32) + send(given, CORE_PAIRS).astype(jnp.float32)).astype(jnp.bfloat16)
    part, out_0 = beside(lambda x: scatter_stage(x, 0, mine[0]), part, *works[0])
    part = scatter_stage(part, 1, mine[1])
    part = reduce_stage(part, 2)
    part, out_1 = beside(lambda x: gather_stage(x, 1, mine[1]), part, *works[1])
    part, out_2 = beside(lambda x: gather_stage(x, 0, mine[0]), part, *works[2])
    return part, send(part, CORE_PAIRS), out_0, out_1, out_2


def partner(at, count, pairing):
    other = at + 1 if at % 2 == pairing else at - 1
    return other if 0 <= other < count else None


def swap_pairs(row_pairing, col_pairing):
    pairs = []
    for row in range(ROWS):
        for col in range(COLS):
            to_row = row if row_pairing is None else partner(row, ROWS, row_pairing)
            to_col = col if col_pairing is None else partner(col, COLS, col_pairing)
            if to_row is not None and to_col is not None:
                pairs.append((row * COLS + col, to_row * COLS + to_col))
    return pairs


def iota(shape, dim):
    return lax.broadcasted_iota(jnp.int32, shape, dim)


def picks(shape, pairs):
    rows, cols = iota(shape, 0), iota(shape, 1)
    hit = jnp.zeros(shape, jnp.bool_)
    for row, col in pairs:
        hit = hit | ((rows == row) & (cols == col))
    return hit.astype(jnp.float32).astype(jnp.bfloat16)


def dot(a, b, a_dim=1, b_dim=0):
    return lax.dot_general(
        a, b, (((a_dim,), (b_dim,)), ((), ())), preferred_element_type=jnp.float32
    )


def keep(gate, value):
    return jnp.where(gate > 0, value, jnp.zeros_like(value))


def prep_kernel(
    parity, grad, joined, unit_fine, inner_fine, unit_mid, inner_mid, unit_coarse, inner_coarse, lift_mid, lift_coarse,
    fine, mid, coarse, row_0, row_1, col_0, col_1, lift, upstream, gate_mid, in_fine, in_mid,
):
    above = keep(joined[...], grad[...])
    upstream[...] = jnp.transpose(above, (1, 0, 2)).reshape(CELLS, 256)
    fine[...] = jnp.transpose(keep(unit_fine[...], above), (1, 0, 2)).reshape(CELLS, 256)
    gate_mid[...] = jnp.transpose(unit_mid[...], (1, 0, 2)).reshape(CELLS, 128)
    in_fine[...] = jnp.transpose(inner_fine[...], (1, 0, 2)).reshape(CELLS, 256)
    in_mid[...] = jnp.transpose(inner_mid[...], (1, 0, 2)).reshape(CELLS, 128)

    cells, target = iota((256, 192), 0), iota((256, 192), 1)
    pooling = jnp.where(target < 128, cells // 2, cells // 4 + 128) == target
    pooling = pooling.astype(jnp.float32).astype(jnp.bfloat16)
    sum_mid = jnp.zeros((FINE, MID), jnp.float32)
    sum_coarse = jnp.zeros((FINE, COARSE), jnp.float32)
    for row in range(COARSE_ROWS):
        pooled = dot(upstream[row * 192 : (row + 1) * 192, :], pooling)
        quarter = [pooled[k * FINE : (k + 1) * FINE] for k in range(4)]
        for half in range(2):
            cell = (quarter[2 * half] + quarter[2 * half + 1])[:, :128].astype(jnp.bfloat16)
            rows = slice((2 * row + half) * MID, (2 * row + half + 1) * MID)
            gate = gate_mid[rows, :]
            mid[rows, :] = keep(gate, dot(lift_mid[...], cell, 0, 0).astype(jnp.bfloat16))
            sum_mid += dot(cell, gate, 1, 1)
        cell = ((quarter[0] + quarter[1]) + (quarter[2] + quarter[3]))[:, 128:].astype(jnp.bfloat16)
        gate = unit_coarse[row]
        coarse[row] = keep(gate, dot(cell, lift_coarse[...], 0, 0).astype(jnp.bfloat16))
        sum_coarse += dot(cell, gate)

    lift[...] = jnp.zeros(lift.shape, lift.dtype)
    lift[0:48, 0:96] = sum_mid.astype(jnp.bfloat16)
    lift[48:96, 0:64] = sum_coarse[:, 128:].astype(jnp.bfloat16)
    lift[96:144, :] = sum_coarse[:, :128].astype(jnp.bfloat16)

    edges = (
        dot(picks((32, 256), ((0, 0), (1, 1), (16, 254), (17, 255))), fine[...], 1, 1)
        + dot(picks((32, 256), ((2, 0), (18, 255))), in_fine[...], 1, 1)
        + dot(picks((32, 128), ((3, 0), (4, 1), (19, 126), (20, 127))), mid[...], 1, 1)
        + dot(picks((32, 128), ((5, 0), (21, 127))), in_mid[...], 1, 1)
    ).astype(jnp.bfloat16)
    masked = coarse[...].reshape(COARSE_ROWS * COARSE_COLS, COARSE)
    inner = inner_coarse[...].reshape(COARSE_ROWS * COARSE_COLS, COARSE)
    sides = []
    for side, cols in ((0, (0, 1, 0)), (1, (62, 63, 63))):
        row, cell = iota((32, 512), 0), iota((32, 512), 1)
        here = cell - (row % 8) * 64
        first = ((row < 8) & (here == cols[0])) | ((row >= 8) & (row < 16) & (here == cols[1]))
        second = (row >= 16) & (row < 24) & (here == cols[2])
        rim = dot(first.astype(jnp.float32).astype(jnp.bfloat16), masked) + dot(
            second.astype(jnp.float32).astype(jnp.bfloat16), inner
        )
        sides.append((edges[side * 16 : (side + 1) * 16], rim.astype(jnp.bfloat16)))
    for out, to_right in ((col_0, parity[1] == 0), (col_1, parity[1] == 1)):
        edge = jnp.where(to_right, sides[1][0], sides[0][0])
        rim = jnp.where(to_right, sides[1][1], sides[0][1])
        for tile in range(12):
            out[tile * 16 : (tile + 1) * 16, :] = edge[:, tile * 128 : (tile + 1) * 128]
        out[192:224, :] = rim[:, :128]
        out[224:256, :] = jnp.zeros((32, 128), jnp.bfloat16)
        out[224:256, 0:64] = rim[:, 128:]

    for out, last in ((row_0, parity[0] == 0), (row_1, parity[0] == 1)):

        def rim_rows(size):
            return pl.ds(pl.multiple_of(jnp.where(last, CELLS - size, 0), 16), size)

        out[0:96, :] = fine[rim_rows(2 * FINE), 0:128]
        out[96:192, :] = fine[rim_rows(2 * FINE), 128:256]
        out[192:240, :] = in_fine[rim_rows(FINE), 0:128]
        out[240:288, :] = in_fine[rim_rows(FINE), 128:256]
        out[288:480, :] = mid[rim_rows(2 * MID), :]
        out[480:576, :] = in_mid[rim_rows(MID), :]
        pair = coarse[pl.ds(jnp.where(last, 6, 0), 2)].reshape(128, COARSE)
        out[576:704, :] = pair[:, :128]
        single = inner_coarse[pl.ds(jnp.where(last, 7, 0), 1)].reshape(64, COARSE)
        out[704:768, :] = single[:, :128]
        out[768:896, :] = jnp.zeros((128, 128), jnp.bfloat16)
        out[768:896, 0:64] = pair[:, 128:]
        out[768:832, 64:128] = single[:, 128:]


IN_SMEM = pl.BlockSpec(memory_space=pltpu.SMEM)
IN_VMEM = pl.BlockSpec(memory_space=pltpu.VMEM)


class Halo:
    def __init__(self, parity, row_0, row_1, col_0, col_1):
        row_even, col_even = parity[0] == 0, parity[1] == 0
        rows, cols = (row_0[...], row_1[...]), (col_0[...], col_1[...])
        self.top, self.bottom = jnp.where(row_even, rows[1], rows[0]), jnp.where(row_even, rows[0], rows[1])
        self.left, self.right = jnp.where(col_even, cols[1], cols[0]), jnp.where(col_even, cols[0], cols[1])


def corner_kernel(parity, row_0, row_1, side_0, side_1, col_0, col_1):
    half = jnp.bfloat16
    row_even = parity[0] == 0
    halos = (jnp.where(row_even, row_1[...], row_0[...]), jnp.where(row_even, row_0[...], row_1[...]))
    wide = jnp.concatenate(
        [
            jnp.concatenate([jnp.concatenate([rim[576:704, :], rim[768:896, 0:64]], axis=1),
                             jnp.concatenate([rim[704:768, :], rim[768:832, 64:128]], axis=1)], axis=0)
            for rim in halos
        ],
        axis=0,
    )
    sides = []
    for (first, second, single), starts in (((0, 1, 0), (0, 192)), ((126, 127, 127), (96, 240))):
        parts = []
        for rim in halos:
            edge = (
                dot(picks((16, 128), ((0, first), (1, second))), rim[starts[0] : starts[0] + 256], 1, 1)
                + dot(picks((16, 128), ((2, single),)), rim[starts[1] : starts[1] + 256], 1, 1)
                + dot(picks((16, 128), ((3, first), (4, second))), rim[288:544], 1, 1)
                + dot(picks((16, 128), ((5, single),)), rim[480:736], 1, 1)
            ).astype(half)
            parts += [edge[:, :128], edge[:, 128:]]
        first, second, single = (0, 1, 0) if first == 0 else (62, 63, 63)
        pairs = []
        for index, at in ((0, 0), (5, 192)):
            pairs += [(index, at + first), (index + 1, at + second), (index + 2, at + 64 + first), (index + 3, at + 64 + second)]
            pairs.append((index + 4, at + 128 + single))
        rim = dot(picks((16, 384), pairs), wide).astype(half)
        parts += [rim[:, :128], jnp.concatenate([rim[:, 128:], jnp.zeros((16, 64), half)], axis=1)]
        sides.append(jnp.concatenate(parts, axis=0))
    for out, side, to_right in ((col_0, side_0, parity[1] == 0), (col_1, side_1, parity[1] == 1)):
        out[0:256, :] = side[...]
        out[256:352, :] = jnp.where(to_right, sides[1], sides[0])


def corners(parity, *messages):
    return pl.pallas_call(
        corner_kernel,
        out_shape=[jax.ShapeDtypeStruct((352, 128), jnp.bfloat16)] * 2,
        in_specs=[IN_SMEM] + [IN_VMEM] * 4,
        compiler_params=PARAMS,
        name="corners",
    )(parity, *messages)


def prep(*args):
    half = jnp.bfloat16
    shapes = (
        (CELLS, 256), (CELLS, 128), (COARSE_ROWS, COARSE_COLS, COARSE),
        (896, 128), (896, 128), (256, 128), (256, 128), (144, 128),
    )
    return pl.pallas_call(
        prep_kernel,
        out_shape=[jax.ShapeDtypeStruct(shape, half) for shape in shapes],
        in_specs=[IN_SMEM] + [IN_VMEM] * 10,
        scratch_shapes=[pltpu.VMEM((CELLS, width), half) for width in (256, 128, 256, 128)],
        compiler_params=PARAMS,
        name="prep",
    )(*args)


def channel_part(halo, second, refs, write_px, *, chans, rows, width, edge, fill_rows):
    source, inner, px, mx, ix, sx, acc_first, acc_second = refs
    ring = width + 128
    half = jnp.bfloat16

    ix[chans : chans + CELLS, 0:width] = jnp.transpose(inner[...], (1, 0, 2)).reshape(CELLS, width)
    sx[...] = jnp.transpose(source[...], (1, 0, 2)).reshape(CELLS, width)
    fill_rows(mx, ix, halo.top, 0, 0)
    fill_rows(mx, ix, halo.bottom, 2 * chans + CELLS, chans + CELLS)
    place = picks(
        (32, 256),
        ((edge, 0), (edge + 1, 1), (16 + edge, 126), (17 + edge, 127), (edge + 2, 128), (18 + edge, 255)),
    )

    def columns(right, left, tile):
        rows16 = slice(tile * 16, (tile + 1) * 16)
        both = jnp.concatenate([right[rows16, :], left[rows16, :]], axis=0)
        return dot(both, place, 0, 0).astype(half)

    for tile in range(12):
        cols = columns(halo.right, halo.left, tile)
        mx[2 * chans + tile * 128 : 2 * chans + (tile + 1) * 128, width:ring] = cols[:, :128]
        ix[chans + tile * 128 : chans + (tile + 1) * 128, width:ring] = cols[:, 128:]
    for tile in range(-(-2 * chans // 128)):
        size = min(128, 2 * chans - tile * 128)
        for first_tile, at, inner_at in ((16, 0, 0), (18, 2 * chans + CELLS, chans + CELLS)):
            cols = columns(halo.right, halo.left, first_tile + tile)
            mx[at + tile * 128 : at + tile * 128 + size, width:ring] = cols[:size, :128]
            if tile == 0:
                ix[inner_at : inner_at + chans, width:ring] = cols[:chans, 128:]

    def before(row, carry):
        at = pl.multiple_of(row * chans, 16)
        inner_grad = ring_taps(second[...], mx[pl.ds(at, 3 * chans), :], chans, ring)
        px[pl.ds(at, chans), :] = keep(ix[pl.ds(at, chans), :].astype(jnp.float32), inner_grad).astype(half)
        return carry

    lax.fori_loop(0, rows + 2, before, 0, unroll=True)
    write_px()

    def spread(tile):
        wide = jnp.concatenate([tile.astype(jnp.float32), jnp.zeros((chans, 128), jnp.float32)], axis=1)
        return jnp.concatenate([pltpu.roll(wide, 1, 1), wide, pltpu.roll(wide, ring - 1, 1)], axis=0).astype(half)

    acc_first[...] = jnp.zeros(acc_first.shape, jnp.float32)
    acc_second[...] = jnp.zeros(acc_second.shape, jnp.float32)

    def after(row, carry):
        at = pl.multiple_of(row * chans, 16)
        window = px[pl.ds(at, 3 * chans), :]
        acc_first[...] += dot(spread(sx[pl.ds(at, chans), :]), window, 1, 1)
        own = ix[pl.ds(pl.multiple_of(at + chans, 16), chans), 0:width]
        acc_second[...] += dot(spread(own), mx[pl.ds(pl.multiple_of(at + chans, 16), 3 * chans), :], 1, 1)
        return carry

    lax.fori_loop(0, rows, after, 0, unroll=True)


def ring_taps(weight, window, chans, ring):
    parts = dot(weight, window)
    return pltpu.roll(parts[:chans], ring - 1, 1) + parts[chans : 2 * chans] + pltpu.roll(parts[2 * chans :], 1, 1)


def input_kernel(masked, px, first, out, ox, *, chans, rows, width):
    def step(row, carry):
        at = pl.multiple_of(row * chans, 16)
        grad = ring_taps(first[...], px[pl.ds(at, 3 * chans), :], chans, width + 128)[:, :width]
        ox[pl.ds(row, 1), :, :] = (masked[pl.ds(at, chans), :].astype(jnp.float32) + grad).astype(jnp.bfloat16)[None]
        return carry

    lax.fori_loop(0, rows, step, 0, unroll=True)
    out[...] = jnp.transpose(ox[...], (1, 0, 2))


def fine_rows(mx, ix, halo, at, inner_at):
    mx[at : at + 96, 0:128] = halo[0:96, :]
    mx[at : at + 96, 128:256] = halo[96:192, :]
    ix[inner_at : inner_at + 48, 0:128] = halo[192:240, :]
    ix[inner_at : inner_at + 48, 128:256] = halo[240:288, :]


def mid_rows(mx, ix, halo, at, inner_at):
    mx[at : at + 192, 0:128] = halo[288:480, :]
    ix[inner_at : inner_at + 96, 0:128] = halo[480:576, :]


def fine_grads(grads, acc_first, acc_second):
    for tap in range(3):
        cols = slice((2 - tap) * FINE, (3 - tap) * FINE)
        pair = jnp.concatenate([acc_second[:, cols], acc_first[:, cols], jnp.zeros((144, 32), jnp.float32)], axis=1)
        grads[tap * 144 : (tap + 1) * 144, :] = pair.astype(jnp.bfloat16)


def mid_grads(grads, acc_first, acc_second):
    for index, acc in enumerate((acc_second, acc_first)):
        for tap in range(3):
            part = jnp.concatenate(
                [acc[:, (2 - tap) * MID : (3 - tap) * MID], jnp.zeros((288, 32), jnp.float32)], axis=1
            )
            at = (3 * index + tap) * 288
            grads[at : at + 288, :] = part.astype(jnp.bfloat16)


def stacked(weight, chans):
    return jnp.transpose(weight[::-1], (1, 2, 0, 3)).reshape(3 * chans, 3 * chans)


def channel_input(masked, px, first, chans, rows, width, name):
    def kernel(*refs):
        input_kernel(*refs, chans=chans, rows=rows, width=width)

    return pl.pallas_call(
        kernel,
        out_shape=jax.ShapeDtypeStruct((chans, rows, width), jnp.bfloat16),
        scratch_shapes=[pltpu.VMEM((rows, chans, width), jnp.bfloat16)],
        compiler_params=PARAMS,
        name=name,
    )(masked, px, stacked(first, chans))


def coarse_places():
    place = np.zeros((2, 13 * 16, 96), np.float32)
    for index, first_row, count, sides in ((0, -2, 12, ((0, 0, "r"), (1, 1, "r"), (14, 0, "l"), (15, 1, "l"))), (1, -1, 10, ((0, 2, "r"), (15, 2, "l")))):
        for block in range(count + 1):
            for at, which, side in sides:
                row = first_row + block - (1 if side == "r" else 0)
                if row < first_row or row >= first_row + count:
                    continue
                if 0 <= row < 8:
                    source = (0 if side == "r" else 32) + which * 8 + row
                else:
                    source = (64 if side == "r" else 80) + (0 if row < 0 else 5)
                    source += 4 if index else 2 * (row + 2 if row < 0 else row - 8) + which
                place[index, block * 16 + at, source] = 1
    return place.reshape(2 * 13 * 16, 96)


def coarse_taps(ref, weight, start, size):
    total = jnp.zeros((size, COARSE), jnp.float32)
    for row_tap in range(3):
        for col_tap in range(3):
            at = start + (2 - row_tap) * PITCH
            total += dot(ref[col_tap, at : at + size, :], weight[row_tap, col_tap], 1, 1)
    return total


def coarse_part(halo, second, place, refs, write_px):
    source, inner, masked, grads, px, mx, ix, own, turned, tail = refs
    half = jnp.bfloat16
    lead = 16
    rims = jnp.concatenate(
        [jnp.concatenate([rim[192:224, :], rim[224:256, 0:64]], axis=1) for rim in (halo.right, halo.left)]
        + [jnp.concatenate([rim[320:336, :], rim[336:352, 0:64]], axis=1) for rim in (halo.right, halo.left)],
        axis=0,
    )
    rims = dot(place[...], rims).astype(half)

    def rows_of(rim):
        pair = jnp.concatenate([rim[576:704, :], rim[768:896, 0:64]], axis=1)
        single = jnp.concatenate([rim[704:768, :], rim[768:832, 64:128]], axis=1)
        return pair, single

    above, above_inner = rows_of(halo.top)
    below, below_inner = rows_of(halo.bottom)
    grid = [above[:64], above[64:]] + [masked[k] for k in range(8)] + [below[:64], below[64:]]
    inner_grid = [above_inner] + [inner[k] for k in range(8)] + [below_inner]
    for ref, blocks, at in ((mx.at[1], grid, 0), (ix, inner_grid, 208)):
        ref[0:lead, :] = rims[at : at + 16]
        for k, block in enumerate(blocks):
            start = lead + k * PITCH
            ref[start : start + 64, :] = block
            ref[start + 64 : start + PITCH, :] = rims[at + (k + 1) * 16 : at + (k + 2) * 16]

    def shifted(ref, size):
        whole = ref[1].astype(jnp.float32)
        ref[0] = pltpu.roll(whole, size - 1, 0).astype(half)
        ref[2] = pltpu.roll(whole, 1, 0).astype(half)

    shifted(mx, 976)
    for start in range(0, 816, 272):
        inner_grad = coarse_taps(mx, second, start, 272)
        px[1, start : start + 272, :] = keep(
            ix[start : start + 272, :].astype(jnp.float32), inner_grad
        ).astype(half)
    shifted(px, 816)
    write_px()
    def corr(tile, ref, start, write):
        own[...] = jnp.zeros(own.shape, half)
        for row in range(8):
            own[row * PITCH : row * PITCH + 64, :] = tile[row]
        turned[...] = jnp.transpose(own[...].astype(jnp.float32)).astype(half)
        for row_tap in range(3):
            for col_tap in range(3):
                at = start + (2 - row_tap) * PITCH
                write(row_tap * 3 + col_tap, dot(turned[...], ref[col_tap, at : at + 8 * PITCH, :]))

    def write_second(tap, value):
        grads[tap * COARSE : (tap + 1) * COARSE, :] = value[:, :128].astype(half)
        tail[tap * COARSE : (tap + 1) * COARSE, :] = value[:, 128:].astype(half)

    def write_first(tap, value):
        at = 1728 + tap * COARSE
        grads[at : at + COARSE, :] = value[:, :128].astype(half)
        rows = slice(3456 + tap * COARSE, 3456 + (tap + 1) * COARSE)
        grads[rows, :] = jnp.concatenate(
            [tail[tap * COARSE : (tap + 1) * COARSE, :], value[:, 128:].astype(half)], axis=1
        )

    corr(inner, mx, lead + PITCH, write_second)
    corr(source, px, lead, write_first)


def grads_kernel(parity, *refs):
    messages, (second_coarse, second_mid, second_fine, place, lift), refs = refs[:4], refs[4:9], refs[9:]
    arrays, (px_coarse, px_mid, px_fine, kept, given), refs = refs[:9], refs[9:14], refs[14:]
    held, work, (load_sems, px_sems, sum_sems) = refs[:7], refs[7:28], refs[28:]
    coarse_work, mid_work, fine_work = work[:7], work[7:14], work[14:21]
    sum_coarse, sum_mid, sum_fine = coarse_work[0], mid_work[0], fine_work[0]
    mx_mid, mx_fine = mid_work[2], fine_work[2]
    core = parity[0]

    places = (
        *held[:3],
        held[3], held[4], mx_mid.at[2 * MID : 2 * MID + CELLS, 0:128],
        held[5], held[6], mx_fine.at[2 * FINE : 2 * FINE + CELLS, 0:256],
    )
    loads = [pltpu.make_async_copy(array, to, load_sems.at[k]) for k, (array, to) in enumerate(zip(arrays, places))]
    for load in loads:
        load.start()
    halo = Halo(parity, *messages)

    px_copies = [
        pltpu.make_async_copy(work[1], out, px_sems.at[k])
        for k, (work, out) in enumerate(((coarse_work, px_coarse), (mid_work, px_mid), (fine_work, px_fine)))
    ]
    half_rows = SUM_ROWS // 2

    def sum_copies(k, source, at, size):
        start = at % half_rows
        return [pltpu.make_async_copy(source, out.at[start : start + size, :], sum_sems.at[k]) for out in (kept, given)]

    def write(copies, at):
        keeps = core == at // half_rows

        @pl.when(keeps)
        def _():
            copies[0].start()

        @pl.when(jnp.logical_not(keeps))
        def _():
            copies[1].start()

    rest = AT_MID - half_rows
    pieces = (
        (sum_coarse.at[0:half_rows, :], 0, half_rows),
        (sum_coarse.at[half_rows:AT_MID, :], half_rows, rest),
        (sum_mid, AT_MID, AT_FINE - AT_MID),
        (sum_fine, AT_FINE, SUM_ROWS - AT_FINE),
    )
    sums = [sum_copies(k, *piece) for k, piece in enumerate(pieces)]

    for load in loads[:3]:
        load.wait()
    coarse_part(halo, second_coarse, place, (*held[:3], *coarse_work), px_copies[0].start)
    write(sums[0], pieces[0][1])
    write(sums[1], pieces[1][1])

    for load in loads[3:6]:
        load.wait()
    channel_part(
        halo, second_mid, (held[3], held[4], *mid_work[1:]), px_copies[1].start,
        chans=MID, rows=16, width=128, edge=3, fill_rows=mid_rows,
    )
    mid_grads(sum_mid, mid_work[5], mid_work[6])
    write(sums[2], pieces[2][1])

    for load in loads[6:]:
        load.wait()
    channel_part(
        halo, second_fine, (held[5], held[6], *fine_work[1:]), px_copies[2].start,
        chans=FINE, rows=32, width=256, edge=0, fill_rows=fine_rows,
    )
    fine_grads(sum_fine, fine_work[5], fine_work[6])
    sum_fine[432:576, :] = lift[...]
    sum_fine[576:, :] = jnp.zeros((SUM_ROWS - AT_LIFT - 144, 128), jnp.bfloat16)
    write(sums[3], pieces[3][1])

    for copy in px_copies:
        copy.wait()
    for copies in sums:
        copies[0].wait()


def grads(parity, messages, seconds, lift, arrays):
    half = jnp.bfloat16
    any_memory = pl.BlockSpec(memory_space=pl.ANY)
    full = jnp.float32

    def channel_work(chans, rows, width, sum_rows):
        ring = width + 128
        return [
            ((sum_rows, 128), half),
            (((rows + 2) * chans, ring), half),
            (((rows + 4) * chans, ring), half),
            (((rows + 2) * chans, ring), half),
            ((CELLS, width), half),
            ((3 * chans, 3 * chans), full),
            ((3 * chans, 3 * chans), full),
        ]

    tile = ((COARSE_ROWS, COARSE_COLS, COARSE), half)
    held = [tile, tile, tile] + [((MID, 16, 128), half)] * 2 + [((FINE, 32, 256), half)] * 2
    coarse_work = [
        ((AT_MID, 128), half),
        ((3, 816, COARSE), half),
        ((3, 976, COARSE), half),
        ((816, COARSE), half),
        ((8 * PITCH, COARSE), half),
        ((COARSE, 8 * PITCH), half),
        ((1728, 64), half),
    ]
    scratch = held + coarse_work + channel_work(MID, 16, 128, AT_FINE - AT_MID) + channel_work(FINE, 32, 256, SUM_ROWS - AT_FINE)
    return pl.pallas_call(
        grads_kernel,
        out_shape=[
            jax.ShapeDtypeStruct((3, 816, COARSE), half),
            jax.ShapeDtypeStruct((18 * MID, 256), half),
            jax.ShapeDtypeStruct((34 * FINE, 384), half),
            jax.ShapeDtypeStruct((SUM_ROWS // 2, 128), half),
            jax.ShapeDtypeStruct((SUM_ROWS // 2, 128), half),
        ],
        in_specs=[IN_SMEM] + [IN_VMEM] * 9 + [any_memory] * 9,
        out_specs=[any_memory] * 5,
        scratch_shapes=[pltpu.VMEM(*shape) for shape in scratch]
        + [pltpu.SemaphoreType.DMA((9,)), pltpu.SemaphoreType.DMA((3,)), pltpu.SemaphoreType.DMA((4,))],
        compiler_params=PARAMS,
        name="grads",
    )(parity, *messages, *seconds, jnp.asarray(coarse_places(), half), lift, *arrays)


def coarse_input_kernel(masked, px, first, out):
    for start in range(0, 8, 4):
        grad = coarse_taps(px, first, 16 + start * PITCH, 4 * PITCH)
        for row in range(start, start + 4):
            at = (row - start) * PITCH
            out[row] = (masked[row].astype(jnp.float32) + grad[at : at + 64]).astype(jnp.bfloat16)


def coarse_input(masked, px, first):
    return pl.pallas_call(
        coarse_input_kernel,
        out_shape=jax.ShapeDtypeStruct((COARSE_ROWS, COARSE_COLS, COARSE), jnp.bfloat16),
        compiler_params=PARAMS,
        name="coarse_input",
    )(masked, px, first)


def unpack_kernel(parity, kept, other, *refs):
    outs, tiles, sems = refs[:8], refs[8:16], refs[16]
    mine, theirs = kept[...], other[...]
    first_half = parity[0] == 0
    halves = (jnp.where(first_half, mine, theirs), jnp.where(first_half, theirs, mine))
    first_fine, second_fine, first_mid, second_mid, first_coarse, second_coarse, lift_mid, lift_coarse = tiles

    def part(start, size, lanes=slice(0, 128)):
        at = start % 3840
        return halves[start // 3840][at : at + size, lanes].astype(jnp.float32)

    copies = []

    def leave(tile, out):
        copy = pltpu.make_async_copy(tile, out, sems.at[len(copies)])
        copy.start()
        copies.append(copy)

    for tap in range(9):
        row_tap, col_tap = tap // 3, tap % 3
        tails = part(3456 + tap * COARSE, COARSE)
        second_coarse[row_tap, col_tap, :, 0:128] = part(tap * COARSE, COARSE)
        second_coarse[row_tap, col_tap, :, 128:192] = tails[:, :64]
        first_coarse[row_tap, col_tap, :, 0:128] = part(1728 + tap * COARSE, COARSE)
        first_coarse[row_tap, col_tap, :, 128:192] = tails[:, 64:]
        if col_tap == 2:
            leave(second_coarse.at[row_tap], outs[5].at[row_tap])
            leave(first_coarse.at[row_tap], outs[4].at[row_tap])
    for tap in range(9):
        row_tap, col_tap = tap // 3, tap % 3
        second_mid[row_tap, col_tap] = part(AT_MID + tap * MID, MID, slice(0, 96))
        first_mid[row_tap, col_tap] = part(AT_MID + 864 + tap * MID, MID, slice(0, 96))
    leave(second_mid, outs[3])
    leave(first_mid, outs[2])
    for tap in range(9):
        row_tap, col_tap = tap // 3, tap % 3
        pair = part(AT_FINE + tap * FINE, FINE)
        second_fine[row_tap, col_tap] = pair[:, 0:48]
        first_fine[row_tap, col_tap] = pair[:, 48:96]
    leave(second_fine, outs[1])
    leave(first_fine, outs[0])
    lift_mid[...] = part(AT_LIFT, 48, slice(0, 96))
    lift_coarse[:, 0:128] = part(AT_LIFT + 96, 48)
    lift_coarse[:, 128:192] = part(AT_LIFT + 48, 48, slice(0, 64))
    leave(lift_mid, outs[6])
    leave(lift_coarse, outs[7])
    for copy in copies:
        copy.wait()


def unpack(parity, kept, other):
    shapes = ((3, 3, 48, 48),) * 2 + ((3, 3, 96, 96),) * 2 + ((3, 3, 192, 192),) * 2 + ((48, 96), (48, 192))
    *taps, lift_mid, lift_coarse = pl.pallas_call(
        unpack_kernel,
        out_shape=[jax.ShapeDtypeStruct(shape, jnp.float32) for shape in shapes],
        in_specs=[IN_SMEM, IN_VMEM, IN_VMEM],
        out_specs=[pl.BlockSpec(memory_space=pl.ANY)] * 8,
        scratch_shapes=[pltpu.VMEM(shape, jnp.float32) for shape in shapes] + [pltpu.SemaphoreType.DMA((12,))],
        compiler_params=PARAMS,
        name="unpack",
    )(parity, kept, other)
    return *taps, jnp.transpose(lift_mid), jnp.transpose(lift_coarse)


def on_device(
    grad_joined, joined_fine, input_fine, inner_fine, unit_fine, input_mid, inner_mid, unit_mid,
    input_coarse, inner_coarse, unit_coarse, first_fine, second_fine, first_mid, second_mid,
    first_coarse, second_coarse, lift_mid, lift_coarse,
):
    input_coarse, inner_coarse, unit_coarse = (
        jnp.transpose(x, (1, 2, 0)) for x in (input_coarse, inner_coarse, unit_coarse)
    )
    parity = jnp.stack([lax.axis_index("row") % 2, lax.axis_index("col") % 2]).astype(jnp.int32)
    fine, mid, coarse, row_0, row_1, col_0, col_1, lift = prep(
        parity, grad_joined, joined_fine, unit_fine, inner_fine, unit_mid, inner_mid, unit_coarse, inner_coarse,
        jnp.transpose(lift_mid), jnp.transpose(lift_coarse),
    )
    row_0, row_1 = send(row_0, swap_pairs(0, None)), send(row_1, swap_pairs(1, None))
    col_0, col_1 = corners(parity, row_0, row_1, col_0, col_1)
    col_0, col_1 = send(col_0, swap_pairs(None, 0)), send(col_1, swap_pairs(None, 1))
    coarse_px, mid_px, fine_px, kept, given = grads(
        parity,
        (row_0, row_1, col_0, col_1),
        (second_coarse, stacked(second_mid, MID), stacked(second_fine, FINE)),
        lift,
        (input_coarse, inner_coarse, coarse, input_mid, inner_mid, mid, input_fine, inner_fine, fine),
    )
    kept, other, fine_input, mid_input, input_grad = all_sum(
        kept,
        given,
        (
            (lambda px: channel_input(fine, px, first_fine, FINE, 32, 256, "fine_input"), fine_px),
            (lambda px: channel_input(mid, px, first_mid, MID, 16, 128, "mid_input"), mid_px),
            (lambda px: coarse_input(coarse, px, first_coarse), coarse_px),
        ),
    )
    return (fine_input, mid_input, jnp.transpose(input_grad, (2, 0, 1)), *unpack(parity, kept, other))


def solution(mesh):
    tiled = P(None, "row", "col")
    return jax.shard_map(
        on_device,
        mesh=mesh,
        in_specs=(tiled,) * 11 + (P(),) * 8,
        out_specs=(tiled,) * 3 + (P(),) * 8,
        check_vma=False,
    )
```

```python
import jax
import jax.numpy as jnp
import numpy as np
from jax import lax
from jax.experimental import pallas as pl
from jax.experimental.pallas import tpu as pltpu
from jax.sharding import PartitionSpec as P

ROWS, COLS = 32, 4
CELLS = 1536
FINE, MID = 48, 96
COARSE_ROWS, COARSE_COLS, COARSE = 8, 64, 192
PITCH = 80
AT_TAIL, AT_MID, AT_FINE, AT_LIFT, HALF_ROWS = 1728, 2592, 3456, 3744, 3840
PARAMS = pltpu.CompilerParams(vmem_limit_bytes=56 * 2**20)

AXES = ("row", "col")
ORDER = (("y", "x", "z"), ("x", "z", "y"))
CORE_PAIRS = [(d, d ^ 4) for d in range(128)]


def stage_pairs(stage, k):
    pairs = []
    for d in range(128):
        row, col = divmod(d, 4)
        at = {"x": row // 8, "z": (row // 2) % 4, "y": col}
        core = row % 2
        at[ORDER[core][stage]] ^= k
        pairs.append((d, (at["x"] * 8 + at["z"] * 2 + core) * 4 + at["y"]))
    return pairs


def my_place():
    row, col = lax.axis_index("row"), lax.axis_index("col")
    at = {"x": row // 8, "z": (row // 2) % 4, "y": col}
    core = row % 2
    return core, [jnp.where(core == 0, at[ORDER[0][s]], at[ORDER[1][s]]) for s in range(3)]


def send(block, pairs):
    return lax.ppermute(block, AXES, pairs)


def add4(own, others):
    a, b, c = [other.astype(jnp.float32) for other in others]
    return ((own.astype(jnp.float32) + a) + (b + c)).astype(jnp.bfloat16)


def scatter_stage(block, stage, mine):
    parts = block.reshape(4, block.shape[0] // 4, block.shape[1])
    own = lax.dynamic_index_in_dim(parts, mine, 0, keepdims=False)
    others = [
        send(lax.dynamic_index_in_dim(parts, mine ^ k, 0, keepdims=False), stage_pairs(stage, k))
        for k in (1, 2, 3)
    ]
    return add4(own, others)


def reduce_stage(block, stage):
    return add4(block, [send(block, stage_pairs(stage, k)) for k in (1, 2, 3)])


def gather_stage(block, stage, mine):
    parts = [block] + [send(block, stage_pairs(stage, k)) for k in (1, 2, 3)]
    whole = jnp.zeros((4,) + block.shape, block.dtype)
    for k in range(4):
        whole = lax.dynamic_update_index_in_dim(whole, parts[k], mine ^ k, 0)
    return whole.reshape(4 * block.shape[0], block.shape[1])


def beside(stage, block, work, *operands):
    block, *operands = lax.optimization_barrier((block, *operands))
    return lax.optimization_barrier((stage(block), work(*operands)))


def all_sum(kept, given, works, last_work):
    _, mine = my_place()
    part = (kept.astype(jnp.float32) + send(given, CORE_PAIRS).astype(jnp.float32)).astype(jnp.bfloat16)
    part, out_0 = beside(lambda x: scatter_stage(x, 0, mine[0]), part, *works[0])
    part = scatter_stage(part, 1, mine[1])
    part = reduce_stage(part, 2)
    part, out_1 = beside(lambda x: gather_stage(x, 1, mine[1]), part, *works[1])
    part, out_2 = beside(lambda x: gather_stage(x, 0, mine[0]), part, *works[2])
    other, out_3 = beside(lambda x: send(x, CORE_PAIRS), part, last_work, part)
    return other, out_3, out_0, out_1, out_2


def partner(at, count, pairing):
    other = at + 1 if at % 2 == pairing else at - 1
    return other if 0 <= other < count else None


def swap_pairs(row_pairing, col_pairing):
    pairs = []
    for row in range(ROWS):
        for col in range(COLS):
            to_row = row if row_pairing is None else partner(row, ROWS, row_pairing)
            to_col = col if col_pairing is None else partner(col, COLS, col_pairing)
            if to_row is not None and to_col is not None:
                pairs.append((row * COLS + col, to_row * COLS + to_col))
    return pairs


def iota(shape, dim):
    return lax.broadcasted_iota(jnp.int32, shape, dim)


def picks(shape, pairs):
    rows, cols = iota(shape, 0), iota(shape, 1)
    hit = jnp.zeros(shape, jnp.bool_)
    for row, col in pairs:
        hit = hit | ((rows == row) & (cols == col))
    return hit.astype(jnp.float32).astype(jnp.bfloat16)


def dot(a, b, a_dim=1, b_dim=0):
    return lax.dot_general(
        a, b, (((a_dim,), (b_dim,)), ((), ())), preferred_element_type=jnp.float32
    )


def keep(gate, value):
    return jnp.where(gate > 0, value, jnp.zeros_like(value))


def my_parity():
    return lax.axis_index("row") % 2, lax.axis_index("col") % 2


def prep_kernel(
    grad, joined, unit_fine, inner_fine, unit_mid, inner_mid, unit_coarse, inner_coarse, lift_mid, lift_coarse,
    fine, mid, coarse, row_0, row_1, pooled_mid, pooled_coarse, upstream, gate_mid, in_fine, in_mid,
):
    step = pl.program_id(0)
    cells = CELLS // 2
    above = keep(joined[...], grad[...])
    upstream[...] = jnp.transpose(above, (1, 0, 2)).reshape(cells, 256)
    fine[...] = jnp.transpose(keep(unit_fine[...], above), (1, 0, 2)).reshape(cells, 256)
    in_fine[...] = jnp.transpose(inner_fine[...], (1, 0, 2)).reshape(cells, 256)

    @pl.when(step == 0)
    def _():
        gate_mid[...] = jnp.transpose(unit_mid[...], (1, 0, 2)).reshape(CELLS, 128)
        in_mid[...] = jnp.transpose(inner_mid[...], (1, 0, 2)).reshape(CELLS, 128)

    source, target = iota((256, 192), 0), iota((256, 192), 1)
    pooling = jnp.where(target < 128, source // 2, source // 4 + 128) == target
    pooling = pooling.astype(jnp.float32).astype(jnp.bfloat16)
    for row in range(COARSE_ROWS // 2):
        pooled = dot(upstream[row * 192 : (row + 1) * 192, :], pooling)
        quarter = [pooled[k * FINE : (k + 1) * FINE] for k in range(4)]
        for half in range(2):
            at = 2 * row + half
            cell = (quarter[2 * half] + quarter[2 * half + 1])[:, :128].astype(jnp.bfloat16)
            pooled_mid[at * FINE : (at + 1) * FINE, :] = cell
            gate = gate_mid[pl.ds(pl.multiple_of(step * cells + at * MID, 16), MID), :]
            mid[at * MID : (at + 1) * MID, :] = keep(gate, dot(lift_mid[...], cell, 0, 0).astype(jnp.bfloat16))
        cell = ((quarter[0] + quarter[1]) + (quarter[2] + quarter[3]))[:, 128:].astype(jnp.bfloat16)
        pooled_coarse[row * FINE : (row + 1) * FINE, :] = cell
        coarse[row] = keep(unit_coarse[row], dot(cell, lift_coarse[...], 0, 0).astype(jnp.bfloat16))

    row_parity, _ = my_parity()
    for out, last in ((row_0, row_parity == 0), (row_1, row_parity == 1)):

        @pl.when(step == last.astype(jnp.int32))
        def _(out=out, last=last):
            def rim_rows(size, whole=cells):
                return pl.ds(pl.multiple_of(jnp.where(last, whole - size, 0), 16), size)

            out[0:96, :] = fine[rim_rows(2 * FINE), 0:128]
            out[96:192, :] = fine[rim_rows(2 * FINE), 128:256]
            out[192:240, :] = in_fine[rim_rows(FINE), 0:128]
            out[240:288, :] = in_fine[rim_rows(FINE), 128:256]
            out[288:480, :] = mid[rim_rows(2 * MID), :]
            out[480:576, :] = in_mid[rim_rows(MID, CELLS), :]
            pair = coarse[pl.ds(jnp.where(last, 2, 0), 2)].reshape(128, COARSE)
            out[576:704, :] = pair[:, :128]
            single = inner_coarse[pl.ds(jnp.where(last, 3, 0), 1)].reshape(64, COARSE)
            out[704:768, :] = single[:, :128]
            out[768:896, :] = jnp.zeros((128, 128), jnp.bfloat16)
            out[768:896, 0:64] = pair[:, 128:]
            out[768:832, 64:128] = single[:, 128:]


def prep(*args):
    half = jnp.bfloat16
    steps = [
        ((CELLS, 256), (CELLS // 2, 256)),
        ((CELLS, 128), (CELLS // 2, 128)),
        ((COARSE_ROWS, COARSE_COLS, COARSE), (COARSE_ROWS // 2, COARSE_COLS, COARSE)),
        ((896, 128), None),
        ((896, 128), None),
        ((16 * FINE, 128), (8 * FINE, 128)),
        ((8 * FINE, 64), (4 * FINE, 64)),
    ]

    def whole(shape):
        return pl.BlockSpec(shape, lambda i: (0,) * len(shape))

    def leading(shape):
        return pl.BlockSpec(shape, lambda i: (i,) + (0,) * (len(shape) - 1))

    tall = pl.BlockSpec((FINE, 16, 256), lambda i: (0, i, 0))
    wide = whole((MID, 16, 128))
    deep = leading((COARSE_ROWS // 2, COARSE_COLS, COARSE))
    return pl.pallas_call(
        prep_kernel,
        grid=(2,),
        out_shape=[jax.ShapeDtypeStruct(shape, half) for shape, _ in steps],
        in_specs=[tall] * 4 + [wide] * 2 + [deep] * 2 + [whole((FINE, MID)), whole((FINE, COARSE))],
        out_specs=[leading(block) if block else whole(shape) for shape, block in steps],
        scratch_shapes=[pltpu.VMEM(shape, half) for shape in ((CELLS // 2, 256), (CELLS, 128), (CELLS // 2, 256), (CELLS, 128))],
        compiler_params=PARAMS,
        name="prep",
    )(*args)


def side_kernel(
    fine, mid, coarse, inner_fine, inner_mid, inner_coarse, unit_mid, unit_coarse, pooled_mid, pooled_coarse,
    side_0, side_1, lift, in_fine, in_mid, gate_mid,
):
    in_fine[...] = jnp.transpose(inner_fine[...], (1, 0, 2)).reshape(CELLS, 256)
    in_mid[...] = jnp.transpose(inner_mid[...], (1, 0, 2)).reshape(CELLS, 128)
    gate_mid[...] = jnp.transpose(unit_mid[...], (1, 0, 2)).reshape(CELLS, 128)
    edges = (
        dot(picks((32, 256), ((0, 0), (1, 1), (16, 254), (17, 255))), fine[...], 1, 1)
        + dot(picks((32, 256), ((2, 0), (18, 255))), in_fine[...], 1, 1)
        + dot(picks((32, 128), ((3, 0), (4, 1), (19, 126), (20, 127))), mid[...], 1, 1)
        + dot(picks((32, 128), ((5, 0), (21, 127))), in_mid[...], 1, 1)
    ).astype(jnp.bfloat16)
    masked = coarse[...].reshape(COARSE_ROWS * COARSE_COLS, COARSE)
    inner = inner_coarse[...].reshape(COARSE_ROWS * COARSE_COLS, COARSE)
    sides = []
    for side, cols in ((0, (0, 1, 0)), (1, (62, 63, 63))):
        row, cell = iota((32, 512), 0), iota((32, 512), 1)
        here = cell - (row % 8) * 64
        first = ((row < 8) & (here == cols[0])) | ((row >= 8) & (row < 16) & (here == cols[1]))
        second = (row >= 16) & (row < 24) & (here == cols[2])
        rim = dot(first.astype(jnp.float32).astype(jnp.bfloat16), masked) + dot(
            second.astype(jnp.float32).astype(jnp.bfloat16), inner
        )
        sides.append((edges[side * 16 : (side + 1) * 16], rim.astype(jnp.bfloat16)))
    _, col_parity = my_parity()
    for out, to_right in ((side_0, col_parity == 0), (side_1, col_parity == 1)):
        edge = jnp.where(to_right, sides[1][0], sides[0][0])
        rim = jnp.where(to_right, sides[1][1], sides[0][1])
        for tile in range(12):
            out[tile * 16 : (tile + 1) * 16, :] = edge[:, tile * 128 : (tile + 1) * 128]
        out[192:224, :] = rim[:, :128]
        out[224:256, :] = jnp.zeros((32, 128), jnp.bfloat16)
        out[224:256, 0:64] = rim[:, 128:]

    sum_mid = jnp.zeros((FINE, MID), jnp.float32)
    for row in range(16):
        sum_mid += dot(pooled_mid[row * FINE : (row + 1) * FINE, :], gate_mid[row * MID : (row + 1) * MID, :], 1, 1)
    sum_coarse = jnp.zeros((FINE, COARSE), jnp.float32)
    for row in range(COARSE_ROWS):
        sum_coarse += dot(pooled_coarse[row * FINE : (row + 1) * FINE, :], unit_coarse[row])
    lift[...] = jnp.zeros(lift.shape, lift.dtype)
    lift[0:48, 0:96] = sum_mid.astype(jnp.bfloat16)
    lift[48:96, 64:128] = sum_coarse[:, 128:].astype(jnp.bfloat16)
    lift[96:144, :] = sum_coarse[:, :128].astype(jnp.bfloat16)


def side(*args):
    half = jnp.bfloat16
    return pl.pallas_call(
        side_kernel,
        out_shape=[jax.ShapeDtypeStruct(shape, half) for shape in ((256, 128), (256, 128), (144, 128))],
        scratch_shapes=[pltpu.VMEM((CELLS, width), half) for width in (256, 128, 128)],
        compiler_params=PARAMS,
        name="side",
    )(*args)


IN_VMEM = pl.BlockSpec(memory_space=pltpu.VMEM)


def near(*arrays):
    return [pltpu.with_memory_space_constraint(array, pltpu.VMEM) for array in arrays]


class Halo:
    def __init__(self, row_0, row_1, col_0, col_1):
        row_parity, col_parity = my_parity()
        row_even, col_even = row_parity == 0, col_parity == 0
        rows, cols = (row_0[...], row_1[...]), (col_0[...], col_1[...])
        self.top, self.bottom = jnp.where(row_even, rows[1], rows[0]), jnp.where(row_even, rows[0], rows[1])
        self.left, self.right = jnp.where(col_even, cols[1], cols[0]), jnp.where(col_even, cols[0], cols[1])


def corner_kernel(row_0, row_1, side_0, side_1, col_0, col_1):
    half = jnp.bfloat16
    row_parity, col_parity = my_parity()
    row_even = row_parity == 0
    halos = (jnp.where(row_even, row_1[...], row_0[...]), jnp.where(row_even, row_0[...], row_1[...]))
    wide = jnp.concatenate(
        [
            jnp.concatenate([jnp.concatenate([rim[576:704, :], rim[768:896, 0:64]], axis=1),
                             jnp.concatenate([rim[704:768, :], rim[768:832, 64:128]], axis=1)], axis=0)
            for rim in halos
        ],
        axis=0,
    )
    sides = []
    for (first, second, single), starts in (((0, 1, 0), (0, 192)), ((126, 127, 127), (96, 240))):
        parts = []
        for rim in halos:
            edge = (
                dot(picks((16, 128), ((0, first), (1, second))), rim[starts[0] : starts[0] + 256], 1, 1)
                + dot(picks((16, 128), ((2, single),)), rim[starts[1] : starts[1] + 256], 1, 1)
                + dot(picks((16, 128), ((3, first), (4, second))), rim[288:544], 1, 1)
                + dot(picks((16, 128), ((5, single),)), rim[480:736], 1, 1)
            ).astype(half)
            parts += [edge[:, :128], edge[:, 128:]]
        first, second, single = (0, 1, 0) if first == 0 else (62, 63, 63)
        pairs = []
        for index, at in ((0, 0), (5, 192)):
            pairs += [(index, at + first), (index + 1, at + second), (index + 2, at + 64 + first), (index + 3, at + 64 + second)]
            pairs.append((index + 4, at + 128 + single))
        rim = dot(picks((16, 384), pairs), wide).astype(half)
        parts += [rim[:, :128], jnp.concatenate([rim[:, 128:], jnp.zeros((16, 64), half)], axis=1)]
        sides.append(jnp.concatenate(parts, axis=0))
    for out, side, to_right in ((col_0, side_0, col_parity == 0), (col_1, side_1, col_parity == 1)):
        out[0:256, :] = side[...]
        out[256:352, :] = jnp.where(to_right, sides[1], sides[0])


def corners(*messages):
    return pl.pallas_call(
        corner_kernel,
        out_shape=[pltpu.VMEM((352, 128), jnp.bfloat16)] * 2,
        out_specs=[IN_VMEM] * 2,
        in_specs=[IN_VMEM] * 4,
        compiler_params=PARAMS,
        name="corners",
    )(*near(*messages[:2]), *messages[2:])


def channel_part(halo, second, refs, write_px, *, chans, rows, width, edge, fill_rows):
    source, inner, px, mx, ix, sx, acc_first, acc_second = refs
    ring = width + 128
    half = jnp.bfloat16

    ix[chans : chans + CELLS, 0:width] = jnp.transpose(inner[...], (1, 0, 2)).reshape(CELLS, width)
    sx[...] = jnp.transpose(source[...], (1, 0, 2)).reshape(CELLS, width)
    fill_rows(mx, ix, halo.top, 0, 0)
    fill_rows(mx, ix, halo.bottom, 2 * chans + CELLS, chans + CELLS)
    place = picks(
        (32, 256),
        ((edge, 0), (edge + 1, 1), (16 + edge, 126), (17 + edge, 127), (edge + 2, 128), (18 + edge, 255)),
    )

    def columns(right, left, tile):
        rows16 = slice(tile * 16, (tile + 1) * 16)
        both = jnp.concatenate([right[rows16, :], left[rows16, :]], axis=0)
        return dot(both, place, 0, 0).astype(half)

    for tile in range(12):
        cols = columns(halo.right, halo.left, tile)
        mx[2 * chans + tile * 128 : 2 * chans + (tile + 1) * 128, width:ring] = cols[:, :128]
        ix[chans + tile * 128 : chans + (tile + 1) * 128, width:ring] = cols[:, 128:]
    for tile in range(-(-2 * chans // 128)):
        size = min(128, 2 * chans - tile * 128)
        for first_tile, at, inner_at in ((16, 0, 0), (18, 2 * chans + CELLS, chans + CELLS)):
            cols = columns(halo.right, halo.left, first_tile + tile)
            mx[at + tile * 128 : at + tile * 128 + size, width:ring] = cols[:size, :128]
            if tile == 0:
                ix[inner_at : inner_at + chans, width:ring] = cols[:chans, 128:]

    def before(row, carry):
        at = pl.multiple_of(row * chans, 16)
        inner_grad = ring_taps(second[...], mx[pl.ds(at, 3 * chans), :], chans, ring)
        px[pl.ds(at, chans), :] = keep(ix[pl.ds(at, chans), :].astype(jnp.float32), inner_grad).astype(half)
        return carry

    lax.fori_loop(0, rows + 2, before, 0, unroll=True)
    write_px()

    def spread(tile):
        wide = jnp.concatenate([tile.astype(jnp.float32), jnp.zeros((chans, 128), jnp.float32)], axis=1)
        return jnp.concatenate([pltpu.roll(wide, 1, 1), wide, pltpu.roll(wide, ring - 1, 1)], axis=0).astype(half)

    acc_first[...] = jnp.zeros(acc_first.shape, jnp.float32)
    acc_second[...] = jnp.zeros(acc_second.shape, jnp.float32)

    def after(row, carry):
        at = pl.multiple_of(row * chans, 16)
        window = px[pl.ds(at, 3 * chans), :]
        acc_first[...] += dot(spread(sx[pl.ds(at, chans), :]), window, 1, 1)
        own = ix[pl.ds(pl.multiple_of(at + chans, 16), chans), 0:width]
        acc_second[...] += dot(spread(own), mx[pl.ds(pl.multiple_of(at + chans, 16), 3 * chans), :], 1, 1)
        return carry

    lax.fori_loop(0, rows, after, 0, unroll=True)


def ring_taps(weight, window, chans, ring):
    parts = dot(weight, window)
    return pltpu.roll(parts[:chans], ring - 1, 1) + parts[chans : 2 * chans] + pltpu.roll(parts[2 * chans :], 1, 1)


def input_kernel(masked, px, first, out, ox, *, chans, rows, width):
    def step(row, carry):
        at = pl.multiple_of(row * chans, 16)
        grad = ring_taps(first[...], px[pl.ds(at, 3 * chans), :], chans, width + 128)[:, :width]
        ox[pl.ds(row, 1), :, :] = (masked[pl.ds(at, chans), :].astype(jnp.float32) + grad).astype(jnp.bfloat16)[None]
        return carry

    lax.fori_loop(0, rows, step, 0, unroll=True)
    out[...] = jnp.transpose(ox[...], (1, 0, 2))


def fine_rows(mx, ix, halo, at, inner_at):
    mx[at : at + 96, 0:128] = halo[0:96, :]
    mx[at : at + 96, 128:256] = halo[96:192, :]
    ix[inner_at : inner_at + 48, 0:128] = halo[192:240, :]
    ix[inner_at : inner_at + 48, 128:256] = halo[240:288, :]


def mid_rows(mx, ix, halo, at, inner_at):
    mx[at : at + 192, 0:128] = halo[288:480, :]
    ix[inner_at : inner_at + 96, 0:128] = halo[480:576, :]


def fine_grads(sums, acc_first, acc_second, lift):
    full, half = jnp.float32, jnp.bfloat16
    for index, acc in enumerate((acc_second, acc_first)):
        taps = [acc[:, (2 - tap) * FINE : (3 - tap) * FINE] for tap in range(3)]
        gap = jnp.zeros((144, 16), full)
        sums[index, 0:144, :] = jnp.concatenate([taps[0], gap, taps[1], gap], axis=1).astype(half)
        sums[index, 144:288, :] = jnp.concatenate([taps[2], jnp.zeros((144, 80), full)], axis=1).astype(half)
        sums[index, 288:384, :] = jnp.zeros((96, 128), half)
    sums[0, 288:336, :] = lift[0:48, :]
    sums[1, 288:336, :] = lift[96:144, :]
    sums[1, 144:192, 64:128] = lift[48:96, 64:128]


def mid_grads(sums, acc_first, acc_second):
    for index, acc in enumerate((acc_second, acc_first)):
        for tap in range(3):
            part = jnp.concatenate([acc[:, (2 - tap) * MID : (3 - tap) * MID], jnp.zeros((288, 32), jnp.float32)], axis=1)
            sums[index, tap * 288 : (tap + 1) * 288, :] = part.astype(jnp.bfloat16)


def stacked(weight, chans):
    return jnp.transpose(weight[::-1], (1, 2, 0, 3)).reshape(3 * chans, 3 * chans)


def channel_input(masked, px, first, chans, rows, width, name):
    def kernel(*refs):
        input_kernel(*refs, chans=chans, rows=rows, width=width)

    return pl.pallas_call(
        kernel,
        out_shape=jax.ShapeDtypeStruct((chans, rows, width), jnp.bfloat16),
        scratch_shapes=[pltpu.VMEM((rows, chans, width), jnp.bfloat16)],
        compiler_params=PARAMS,
        name=name,
    )(masked, px, stacked(first, chans))


def coarse_places():
    place = np.zeros((2, 13 * 16, 96), np.float32)
    for index, first_row, count, sides in ((0, -2, 12, ((0, 0, "r"), (1, 1, "r"), (14, 0, "l"), (15, 1, "l"))), (1, -1, 10, ((0, 2, "r"), (15, 2, "l")))):
        for block in range(count + 1):
            for at, which, side in sides:
                row = first_row + block - (1 if side == "r" else 0)
                if row < first_row or row >= first_row + count:
                    continue
                if 0 <= row < 8:
                    source = (0 if side == "r" else 32) + which * 8 + row
                else:
                    source = (64 if side == "r" else 80) + (0 if row < 0 else 5)
                    source += 4 if index else 2 * (row + 2 if row < 0 else row - 8) + which
                place[index, block * 16 + at, source] = 1
    return place.reshape(2 * 13 * 16, 96)


def coarse_taps(ref, weight, start, size):
    total = jnp.zeros((size, COARSE), jnp.float32)
    for row_tap in range(3):
        for col_tap in range(3):
            at = start + (2 - row_tap) * PITCH
            total += dot(ref[col_tap, at : at + size, :], weight[row_tap, col_tap], 1, 1)
    return total


def coarse_part(halo, second, place, refs, write_px):
    source, inner, masked, sums, px, mx, ix, own, turned = refs
    half = jnp.bfloat16
    lead = 16
    rims = jnp.concatenate(
        [jnp.concatenate([rim[192:224, :], rim[224:256, 0:64]], axis=1) for rim in (halo.right, halo.left)]
        + [jnp.concatenate([rim[320:336, :], rim[336:352, 0:64]], axis=1) for rim in (halo.right, halo.left)],
        axis=0,
    )
    rims = dot(place[...], rims).astype(half)

    def rows_of(rim):
        pair = jnp.concatenate([rim[576:704, :], rim[768:896, 0:64]], axis=1)
        single = jnp.concatenate([rim[704:768, :], rim[768:832, 64:128]], axis=1)
        return pair, single

    above, above_inner = rows_of(halo.top)
    below, below_inner = rows_of(halo.bottom)
    grid = [above[:64], above[64:]] + [masked[k] for k in range(8)] + [below[:64], below[64:]]
    inner_grid = [above_inner] + [inner[k] for k in range(8)] + [below_inner]
    for ref, blocks, at in ((mx.at[1], grid, 0), (ix, inner_grid, 208)):
        ref[0:lead, :] = rims[at : at + 16]
        for k, block in enumerate(blocks):
            start = lead + k * PITCH
            ref[start : start + 64, :] = block
            ref[start + 64 : start + PITCH, :] = rims[at + (k + 1) * 16 : at + (k + 2) * 16]

    def shifted(ref, size):
        whole = ref[1].astype(jnp.float32)
        ref[0] = pltpu.roll(whole, size - 1, 0).astype(half)
        ref[2] = pltpu.roll(whole, 1, 0).astype(half)

    shifted(mx, 976)
    for start in range(0, 816, 272):
        inner_grad = coarse_taps(mx, second, start, 272)
        px[1, start : start + 272, :] = keep(
            ix[start : start + 272, :].astype(jnp.float32), inner_grad
        ).astype(half)
    shifted(px, 816)
    write_px()
    def corr(tile, ref, start, write):
        own[...] = jnp.zeros(own.shape, half)
        for row in range(8):
            own[row * PITCH : row * PITCH + 64, :] = tile[row]
        turned[...] = jnp.transpose(own[...].astype(jnp.float32)).astype(half)
        for row_tap in range(3):
            for col_tap in range(3):
                at = start + (2 - row_tap) * PITCH
                write(row_tap * 3 + col_tap, dot(turned[...], ref[col_tap, at : at + 8 * PITCH, :]))

    def writer(index):
        def write(tap, value):
            sums[index, tap * COARSE : (tap + 1) * COARSE, :] = value[:, :128].astype(half)
            tail = jnp.concatenate([value[:96, 128:], value[96:, 128:]], axis=1)
            sums[index, AT_TAIL + tap * 96 : AT_TAIL + (tap + 1) * 96, :] = tail.astype(half)

        return write

    corr(inner, mx, lead + PITCH, writer(0))
    corr(source, px, lead, writer(1))


def grads_kernel(*refs):
    messages, (second_coarse, second_mid, second_fine, place, lift), refs = refs[:4], refs[4:9], refs[9:]
    arrays, (px_coarse, px_mid, px_fine, kept, given), refs = refs[:9], refs[9:14], refs[14:]
    held, work, (load_sems, px_sems, sum_sems) = refs[:7], refs[7:27], refs[27:]
    coarse_work, mid_work, fine_work = work[:6], work[6:13], work[13:20]
    sum_coarse, sum_mid, sum_fine = coarse_work[0], mid_work[0], fine_work[0]
    mx_mid, mx_fine = mid_work[2], fine_work[2]
    core, _ = my_parity()

    places = (
        *held[:3],
        held[3], held[4], mx_mid.at[2 * MID : 2 * MID + CELLS, 0:128],
        held[5], held[6], mx_fine.at[2 * FINE : 2 * FINE + CELLS, 0:256],
    )
    loads = [pltpu.make_async_copy(array, to, load_sems.at[k]) for k, (array, to) in enumerate(zip(arrays, places))]
    for load in loads:
        load.start()
    halo = Halo(*messages)

    px_copies = [
        pltpu.make_async_copy(work[1], out, px_sems.at[k])
        for k, (work, out) in enumerate(((coarse_work, px_coarse), (mid_work, px_mid), (fine_work, px_fine)))
    ]
    def sum_copies(work, start, size, k):
        return [
            [pltpu.make_async_copy(work.at[half], out.at[start : start + size, :], sum_sems.at[2 * k + half]) for out in (kept, given)]
            for half in range(2)
        ]

    def write(copies):
        for half in range(2):
            keeps = core == half

            @pl.when(keeps)
            def _(half=half):
                copies[half][0].start()

            @pl.when(jnp.logical_not(keeps))
            def _(half=half):
                copies[half][1].start()

    pieces = ((sum_coarse, 0, AT_MID), (sum_mid, AT_MID, AT_FINE - AT_MID), (sum_fine, AT_FINE, HALF_ROWS - AT_FINE))
    sums = [sum_copies(*piece, k) for k, piece in enumerate(pieces)]

    for load in loads[:3]:
        load.wait()
    coarse_part(halo, second_coarse, place, (*held[:3], *coarse_work), px_copies[0].start)
    write(sums[0])

    for load in loads[3:6]:
        load.wait()
    channel_part(
        halo, second_mid, (held[3], held[4], *mid_work[1:]), px_copies[1].start,
        chans=MID, rows=16, width=128, edge=3, fill_rows=mid_rows,
    )
    mid_grads(sum_mid, mid_work[5], mid_work[6])
    write(sums[1])

    for load in loads[6:]:
        load.wait()
    channel_part(
        halo, second_fine, (held[5], held[6], *fine_work[1:]), px_copies[2].start,
        chans=FINE, rows=32, width=256, edge=0, fill_rows=fine_rows,
    )
    fine_grads(sum_fine, fine_work[5], fine_work[6], lift)
    write(sums[2])

    for copy in px_copies:
        copy.wait()
    for halves in sums:
        for copies in halves:
            copies[0].wait()


def grads(messages, seconds, lift, arrays):
    half = jnp.bfloat16
    any_memory = pl.BlockSpec(memory_space=pl.ANY)
    full = jnp.float32

    def channel_work(chans, rows, width, sum_rows):
        ring = width + 128
        return [
            ((2, sum_rows, 128), half),
            (((rows + 2) * chans, ring), half),
            (((rows + 4) * chans, ring), half),
            (((rows + 2) * chans, ring), half),
            ((CELLS, width), half),
            ((3 * chans, 3 * chans), full),
            ((3 * chans, 3 * chans), full),
        ]

    tile = ((COARSE_ROWS, COARSE_COLS, COARSE), half)
    held = [tile, tile, tile] + [((MID, 16, 128), half)] * 2 + [((FINE, 32, 256), half)] * 2
    coarse_work = [
        ((2, AT_MID, 128), half),
        ((3, 816, COARSE), half),
        ((3, 976, COARSE), half),
        ((816, COARSE), half),
        ((8 * PITCH, COARSE), half),
        ((COARSE, 8 * PITCH), half),
    ]
    scratch = held + coarse_work + channel_work(MID, 16, 128, AT_FINE - AT_MID) + channel_work(FINE, 32, 256, HALF_ROWS - AT_FINE)
    return pl.pallas_call(
        grads_kernel,
        out_shape=[
            jax.ShapeDtypeStruct((3, 816, COARSE), half),
            jax.ShapeDtypeStruct((18 * MID, 256), half),
            jax.ShapeDtypeStruct((34 * FINE, 384), half),
            jax.ShapeDtypeStruct((HALF_ROWS, 128), half),
            pltpu.VMEM((HALF_ROWS, 128), half),
        ],
        in_specs=[IN_VMEM] * 9 + [any_memory] * 9,
        out_specs=[any_memory] * 4 + [IN_VMEM],
        scratch_shapes=[pltpu.VMEM(*shape) for shape in scratch]
        + [pltpu.SemaphoreType.DMA((9,)), pltpu.SemaphoreType.DMA((3,)), pltpu.SemaphoreType.DMA((6,))],
        compiler_params=PARAMS,
        name="grads",
    )(*near(*messages), *seconds, jnp.asarray(coarse_places(), half), lift, *arrays)


def coarse_input_kernel(masked, px, first, out):
    for start in range(0, 8, 4):
        grad = coarse_taps(px, first, 16 + start * PITCH, 4 * PITCH)
        for row in range(start, start + 4):
            at = (row - start) * PITCH
            out[row] = (masked[row].astype(jnp.float32) + grad[at : at + 64]).astype(jnp.bfloat16)


def coarse_input(masked, px, first):
    return pl.pallas_call(
        coarse_input_kernel,
        out_shape=jax.ShapeDtypeStruct((COARSE_ROWS, COARSE_COLS, COARSE), jnp.bfloat16),
        compiler_params=PARAMS,
        name="coarse_input",
    )(masked, px, first)


def unpack_kernel(summed, *refs, kept):
    outs, (coarse, mid, fine, lift_mid, lift_coarse, sems) = refs[-14:-6], refs[-6:]
    core, _ = my_parity()
    is_second = core == (0 if kept else 1)
    full = jnp.float32
    copies = []

    def leave(tile, first_out, second_out):
        k = len(copies)
        copies.append(pltpu.make_async_copy(tile, second_out, sems.at[k]))
        other = pltpu.make_async_copy(tile, first_out, sems.at[k])

        @pl.when(is_second)
        def _():
            copies[k].start()

        @pl.when(jnp.logical_not(is_second))
        def _():
            other.start()

    for tap in range(9):
        row_tap, col_tap = tap // 3, tap % 3
        coarse[row_tap, col_tap, :, 0:128] = summed[tap * COARSE : (tap + 1) * COARSE, :].astype(full)
        tail = summed[AT_TAIL + tap * 96 : AT_TAIL + (tap + 1) * 96, :].astype(full)
        coarse[row_tap, col_tap, 0:96, 128:192] = tail[:, :64]
        coarse[row_tap, col_tap, 96:192, 128:192] = tail[:, 64:]
        if col_tap == 2:
            leave(coarse.at[row_tap], outs[4].at[row_tap], outs[5].at[row_tap])
    for tap in range(9):
        mid[tap // 3, tap % 3] = summed[AT_MID + tap * MID : AT_MID + (tap + 1) * MID, 0:96].astype(full)
    leave(mid, outs[2], outs[3])
    for col_tap in range(3):
        rows = slice(AT_FINE + col_tap * FINE, AT_FINE + (col_tap + 1) * FINE)
        pair = summed[rows, :].astype(full)
        fine[0, col_tap] = pair[:, 0:48]
        fine[1, col_tap] = pair[:, 64:112]
        rows = slice(AT_FINE + 144 + col_tap * FINE, AT_FINE + 144 + (col_tap + 1) * FINE)
        fine[2, col_tap] = summed[rows, 0:48].astype(full)
    leave(fine, outs[0], outs[1])
    lift_mid[...] = summed[AT_LIFT : AT_LIFT + 48, 0:96].astype(full)
    lift_coarse[:, 0:128] = summed[AT_LIFT : AT_LIFT + 48, :].astype(full)
    lift_coarse[:, 128:192] = summed[AT_FINE + 144 : AT_FINE + 192, 64:128].astype(full)
    lift_copies = [
        pltpu.make_async_copy(tile, out, sems.at[len(copies)]) for tile, out in ((lift_mid, outs[6]), (lift_coarse, outs[7]))
    ]

    @pl.when(is_second)
    def _():
        lift_copies[0].start()
        lift_copies[0].wait()

    @pl.when(jnp.logical_not(is_second))
    def _():
        lift_copies[1].start()
        lift_copies[1].wait()

    for copy in copies:
        copy.wait()


def unpack(summed, earlier=()):
    shapes = ((3, 3, 48, 48),) * 2 + ((3, 3, 96, 96),) * 2 + ((3, 3, 192, 192),) * 2 + ((48, 96), (48, 192))
    any_memory = pl.BlockSpec(memory_space=pl.ANY)

    def kernel(*refs):
        unpack_kernel(*refs, kept=not earlier)

    return pl.pallas_call(
        kernel,
        out_shape=[jax.ShapeDtypeStruct(shape, jnp.float32) for shape in shapes],
        in_specs=[IN_VMEM] + [any_memory] * len(earlier),
        out_specs=[any_memory] * 8,
        scratch_shapes=[pltpu.VMEM(shapes[k], jnp.float32) for k in (4, 2, 0, 6, 7)] + [pltpu.SemaphoreType.DMA((6,))],
        input_output_aliases={k + 1: k for k in range(len(earlier))},
        compiler_params=PARAMS,
        name="unpack_other" if earlier else "unpack_kept",
    )(*near(summed), *earlier)


def on_device(
    grad_joined, joined_fine, input_fine, inner_fine, unit_fine, input_mid, inner_mid, unit_mid,
    input_coarse, inner_coarse, unit_coarse, first_fine, second_fine, first_mid, second_mid,
    first_coarse, second_coarse, lift_mid, lift_coarse,
):
    input_coarse, inner_coarse, unit_coarse = (
        jnp.transpose(x, (1, 2, 0)) for x in (input_coarse, inner_coarse, unit_coarse)
    )
    fine, mid, coarse, row_0, row_1, pooled_mid, pooled_coarse = prep(
        grad_joined, joined_fine, unit_fine, inner_fine, unit_mid, inner_mid, unit_coarse, inner_coarse,
        jnp.transpose(lift_mid), jnp.transpose(lift_coarse),
    )
    row_0, row_1 = send(row_0, swap_pairs(0, None)), send(row_1, swap_pairs(1, None))
    side_0, side_1, lift = side(
        fine, mid, coarse, inner_fine, inner_mid, inner_coarse, unit_mid, unit_coarse, pooled_mid, pooled_coarse
    )
    col_0, col_1 = corners(row_0, row_1, side_0, side_1)
    col_0, col_1 = send(col_0, swap_pairs(None, 0)), send(col_1, swap_pairs(None, 1))
    coarse_px, mid_px, fine_px, kept, given = grads(
        (row_0, row_1, col_0, col_1),
        (second_coarse, stacked(second_mid, MID), stacked(second_fine, FINE)),
        lift,
        (input_coarse, inner_coarse, coarse, input_mid, inner_mid, mid, input_fine, inner_fine, fine),
    )
    other, earlier, fine_input, mid_input, input_grad = all_sum(
        kept,
        given,
        (
            (lambda px: channel_input(fine, px, first_fine, FINE, 32, 256, "fine_input"), fine_px),
            (lambda px: channel_input(mid, px, first_mid, MID, 16, 128, "mid_input"), mid_px),
            (lambda px: coarse_input(coarse, px, first_coarse), coarse_px),
        ),
        unpack,
    )
    *taps, lift_mid, lift_coarse = unpack(other, earlier)
    return (
        fine_input, mid_input, jnp.transpose(input_grad, (2, 0, 1)), *taps, jnp.transpose(lift_mid), jnp.transpose(lift_coarse)
    )


def solution(mesh):
    tiled = P(None, "row", "col")
    return jax.shard_map(
        on_device,
        mesh=mesh,
        in_specs=(tiled,) * 11 + (P(),) * 8,
        out_specs=(tiled,) * 3 + (P(),) * 8,
        check_vma=False,
    )
```

```python
import jax
import jax.numpy as jnp
import numpy as np
from jax import lax
from jax.experimental import pallas as pl
from jax.experimental.pallas import tpu as pltpu
from jax.sharding import PartitionSpec as P

ROWS, COLS = 32, 4
CELLS = 1536
FINE, MID = 48, 96
COARSE_ROWS, COARSE_COLS, COARSE = 8, 64, 192
PITCH = 80
AT_TAIL, AT_MID, AT_FINE, AT_LIFT, HALF_ROWS = 1728, 2592, 3456, 3744, 3840
PARAMS = pltpu.CompilerParams(vmem_limit_bytes=56 * 2**20)

AXES = ("row", "col")
ORDER = (("y", "x", "z"), ("x", "z", "y"))
CORE_PAIRS = [(d, d ^ 4) for d in range(128)]


def stage_pairs(stage, k):
    pairs = []
    for d in range(128):
        row, col = divmod(d, 4)
        at = {"x": row // 8, "z": (row // 2) % 4, "y": col}
        core = row % 2
        at[ORDER[core][stage]] ^= k
        pairs.append((d, (at["x"] * 8 + at["z"] * 2 + core) * 4 + at["y"]))
    return pairs


def my_place():
    row, col = lax.axis_index("row"), lax.axis_index("col")
    at = {"x": row // 8, "z": (row // 2) % 4, "y": col}
    core = row % 2
    return core, [jnp.where(core == 0, at[ORDER[0][s]], at[ORDER[1][s]]) for s in range(3)]


def send(block, pairs):
    return lax.ppermute(block, AXES, pairs)


def add4(own, others):
    a, b, c = [other.astype(jnp.float32) for other in others]
    return ((own.astype(jnp.float32) + a) + (b + c)).astype(jnp.bfloat16)


def scatter_stage(block, stage, mine):
    parts = block.reshape(4, block.shape[0] // 4, block.shape[1])
    own = lax.dynamic_index_in_dim(parts, mine, 0, keepdims=False)
    others = [
        send(lax.dynamic_index_in_dim(parts, mine ^ k, 0, keepdims=False), stage_pairs(stage, k))
        for k in (1, 2, 3)
    ]
    return add4(own, others)


def reduce_stage(block, stage):
    return add4(block, [send(block, stage_pairs(stage, k)) for k in (1, 2, 3)])


def gather_stage(block, stage, mine):
    parts = [block] + [send(block, stage_pairs(stage, k)) for k in (1, 2, 3)]
    whole = jnp.zeros((4,) + block.shape, block.dtype)
    for k in range(4):
        whole = lax.dynamic_update_index_in_dim(whole, parts[k], mine ^ k, 0)
    return whole.reshape(4 * block.shape[0], block.shape[1])


def beside(stage, block, work, *operands):
    block, *operands = lax.optimization_barrier((block, *operands))
    return lax.optimization_barrier((stage(block), work(*operands)))


def all_sum(kept, given, works, last_work):
    _, mine = my_place()
    part = (kept.astype(jnp.float32) + send(given, CORE_PAIRS).astype(jnp.float32)).astype(jnp.bfloat16)
    part, out_0 = beside(lambda x: scatter_stage(x, 0, mine[0]), part, *works[0])
    part = scatter_stage(part, 1, mine[1])
    part = reduce_stage(part, 2)
    part, out_1 = beside(lambda x: gather_stage(x, 1, mine[1]), part, *works[1])
    part, out_2 = beside(lambda x: gather_stage(x, 0, mine[0]), part, *works[2])
    other, out_3 = beside(lambda x: send(x, CORE_PAIRS), part, last_work, part)
    return other, out_3, out_0, out_1, out_2


def partner(at, count, pairing):
    other = at + 1 if at % 2 == pairing else at - 1
    return other if 0 <= other < count else None


def swap_pairs(row_pairing, col_pairing):
    pairs = []
    for row in range(ROWS):
        for col in range(COLS):
            to_row = row if row_pairing is None else partner(row, ROWS, row_pairing)
            to_col = col if col_pairing is None else partner(col, COLS, col_pairing)
            if to_row is not None and to_col is not None:
                pairs.append((row * COLS + col, to_row * COLS + to_col))
    return pairs


def iota(shape, dim):
    return lax.broadcasted_iota(jnp.int32, shape, dim)


def picks(shape, pairs):
    rows, cols = iota(shape, 0), iota(shape, 1)
    hit = jnp.zeros(shape, jnp.bool_)
    for row, col in pairs:
        hit = hit | ((rows == row) & (cols == col))
    return hit.astype(jnp.float32).astype(jnp.bfloat16)


def dot(a, b, a_dim=1, b_dim=0):
    return lax.dot_general(
        a, b, (((a_dim,), (b_dim,)), ((), ())), preferred_element_type=jnp.float32
    )


def keep(gate, value):
    return jnp.where(gate > 0, value, jnp.zeros_like(value))


def my_parity():
    return lax.axis_index("row") % 2, lax.axis_index("col") % 2


def prep_kernel(
    grad, joined, unit_fine, inner_fine, unit_mid, inner_mid, unit_coarse, inner_coarse, lift_mid, lift_coarse,
    fine, mid, coarse, row_0, row_1, pooled_mid, pooled_coarse, upstream, gate_mid, in_fine, in_mid,
):
    step = pl.program_id(0)
    cells = CELLS // 2
    above = keep(joined[...], grad[...])
    upstream[...] = jnp.transpose(above, (1, 0, 2)).reshape(cells, 256)
    fine[...] = jnp.transpose(keep(unit_fine[...], above), (1, 0, 2)).reshape(cells, 256)
    in_fine[...] = jnp.transpose(inner_fine[...], (1, 0, 2)).reshape(cells, 256)

    @pl.when(step == 0)
    def _():
        gate_mid[...] = jnp.transpose(unit_mid[...], (1, 0, 2)).reshape(CELLS, 128)
        in_mid[...] = jnp.transpose(inner_mid[...], (1, 0, 2)).reshape(CELLS, 128)

    source, target = iota((256, 192), 0), iota((256, 192), 1)
    pooling = jnp.where(target < 128, source // 2, source // 4 + 128) == target
    pooling = pooling.astype(jnp.float32).astype(jnp.bfloat16)
    for row in range(COARSE_ROWS // 2):
        pooled = dot(upstream[row * 192 : (row + 1) * 192, :], pooling)
        quarter = [pooled[k * FINE : (k + 1) * FINE] for k in range(4)]
        for half in range(2):
            at = 2 * row + half
            cell = (quarter[2 * half] + quarter[2 * half + 1])[:, :128].astype(jnp.bfloat16)
            pooled_mid[at * FINE : (at + 1) * FINE, :] = cell
            gate = gate_mid[pl.ds(pl.multiple_of(step * cells + at * MID, 16), MID), :]
            mid[at * MID : (at + 1) * MID, :] = keep(gate, dot(lift_mid[...], cell, 0, 0).astype(jnp.bfloat16))
        cell = ((quarter[0] + quarter[1]) + (quarter[2] + quarter[3]))[:, 128:].astype(jnp.bfloat16)
        pooled_coarse[row * FINE : (row + 1) * FINE, :] = cell
        coarse[row] = keep(unit_coarse[row], dot(cell, lift_coarse[...], 0, 0).astype(jnp.bfloat16))

    row_parity, _ = my_parity()
    for out, last in ((row_0, row_parity == 0), (row_1, row_parity == 1)):

        @pl.when(step == last.astype(jnp.int32))
        def _(out=out, last=last):
            def rim_rows(size, whole=cells):
                return pl.ds(pl.multiple_of(jnp.where(last, whole - size, 0), 16), size)

            out[0:96, :] = fine[rim_rows(2 * FINE), 0:128]
            out[96:192, :] = fine[rim_rows(2 * FINE), 128:256]
            out[192:240, :] = in_fine[rim_rows(FINE), 0:128]
            out[240:288, :] = in_fine[rim_rows(FINE), 128:256]
            out[288:480, :] = mid[rim_rows(2 * MID), :]
            out[480:576, :] = in_mid[rim_rows(MID, CELLS), :]
            pair = coarse[pl.ds(jnp.where(last, 2, 0), 2)].reshape(128, COARSE)
            out[576:704, :] = pair[:, :128]
            single = inner_coarse[pl.ds(jnp.where(last, 3, 0), 1)].reshape(64, COARSE)
            out[704:768, :] = single[:, :128]
            out[768:896, :] = jnp.zeros((128, 128), jnp.bfloat16)
            out[768:896, 0:64] = pair[:, 128:]
            out[768:832, 64:128] = single[:, 128:]


def prep(*args):
    half = jnp.bfloat16
    steps = [
        ((CELLS, 256), (CELLS // 2, 256)),
        ((CELLS, 128), (CELLS // 2, 128)),
        ((COARSE_ROWS, COARSE_COLS, COARSE), (COARSE_ROWS // 2, COARSE_COLS, COARSE)),
        ((896, 128), None),
        ((896, 128), None),
        ((16 * FINE, 128), (8 * FINE, 128)),
        ((8 * FINE, 64), (4 * FINE, 64)),
    ]

    def whole(shape):
        return pl.BlockSpec(shape, lambda i: (0,) * len(shape))

    def leading(shape):
        return pl.BlockSpec(shape, lambda i: (i,) + (0,) * (len(shape) - 1))

    tall = pl.BlockSpec((FINE, 16, 256), lambda i: (0, i, 0))
    wide = whole((MID, 16, 128))
    deep = leading((COARSE_ROWS // 2, COARSE_COLS, COARSE))
    return pl.pallas_call(
        prep_kernel,
        grid=(2,),
        out_shape=[jax.ShapeDtypeStruct(shape, half) for shape, _ in steps],
        in_specs=[tall] * 4 + [wide] * 2 + [deep] * 2 + [whole((FINE, MID)), whole((FINE, COARSE))],
        out_specs=[leading(block) if block else whole(shape) for shape, block in steps],
        scratch_shapes=[pltpu.VMEM(shape, half) for shape in ((CELLS // 2, 256), (CELLS, 128), (CELLS // 2, 256), (CELLS, 128))],
        compiler_params=PARAMS,
        name="prep",
    )(*args)


def side_kernel(*refs):
    arrays, outs, scratch, tiles, sems = refs[:10], refs[10:13], refs[13:16], refs[16:26], refs[26]
    pull(arrays, tiles, sems)
    side_work(*tiles, *outs, *scratch)


def pull(arrays, tiles, sems):
    loads = [pltpu.make_async_copy(array, tile, sems.at[k]) for k, (array, tile) in enumerate(zip(arrays, tiles))]
    for load in loads:
        load.start()
    for load in loads:
        load.wait()


def side_work(
    fine, mid, coarse, inner_fine, inner_mid, inner_coarse, unit_mid, unit_coarse, pooled_mid, pooled_coarse,
    side_0, side_1, lift, in_fine, in_mid, gate_mid,
):
    in_fine[...] = jnp.transpose(inner_fine[...], (1, 0, 2)).reshape(CELLS, 256)
    in_mid[...] = jnp.transpose(inner_mid[...], (1, 0, 2)).reshape(CELLS, 128)
    gate_mid[...] = jnp.transpose(unit_mid[...], (1, 0, 2)).reshape(CELLS, 128)
    edges = (
        dot(picks((32, 256), ((0, 0), (1, 1), (16, 254), (17, 255))), fine[...], 1, 1)
        + dot(picks((32, 256), ((2, 0), (18, 255))), in_fine[...], 1, 1)
        + dot(picks((32, 128), ((3, 0), (4, 1), (19, 126), (20, 127))), mid[...], 1, 1)
        + dot(picks((32, 128), ((5, 0), (21, 127))), in_mid[...], 1, 1)
    ).astype(jnp.bfloat16)
    masked = coarse[...].reshape(COARSE_ROWS * COARSE_COLS, COARSE)
    inner = inner_coarse[...].reshape(COARSE_ROWS * COARSE_COLS, COARSE)
    sides = []
    for side, cols in ((0, (0, 1, 0)), (1, (62, 63, 63))):
        row, cell = iota((32, 512), 0), iota((32, 512), 1)
        here = cell - (row % 8) * 64
        first = ((row < 8) & (here == cols[0])) | ((row >= 8) & (row < 16) & (here == cols[1]))
        second = (row >= 16) & (row < 24) & (here == cols[2])
        rim = dot(first.astype(jnp.float32).astype(jnp.bfloat16), masked) + dot(
            second.astype(jnp.float32).astype(jnp.bfloat16), inner
        )
        sides.append((edges[side * 16 : (side + 1) * 16], rim.astype(jnp.bfloat16)))
    _, col_parity = my_parity()
    for out, to_right in ((side_0, col_parity == 0), (side_1, col_parity == 1)):
        edge = jnp.where(to_right, sides[1][0], sides[0][0])
        rim = jnp.where(to_right, sides[1][1], sides[0][1])
        for tile in range(12):
            out[tile * 16 : (tile + 1) * 16, :] = edge[:, tile * 128 : (tile + 1) * 128]
        out[192:224, :] = rim[:, :128]
        out[224:256, :] = jnp.zeros((32, 128), jnp.bfloat16)
        out[224:256, 0:64] = rim[:, 128:]

    sum_mid = jnp.zeros((FINE, MID), jnp.float32)
    for row in range(16):
        sum_mid += dot(pooled_mid[row * FINE : (row + 1) * FINE, :], gate_mid[row * MID : (row + 1) * MID, :], 1, 1)
    sum_coarse = jnp.zeros((FINE, COARSE), jnp.float32)
    for row in range(COARSE_ROWS):
        sum_coarse += dot(pooled_coarse[row * FINE : (row + 1) * FINE, :], unit_coarse[row])
    lift[...] = jnp.zeros(lift.shape, lift.dtype)
    lift[0:48, 0:96] = sum_mid.astype(jnp.bfloat16)
    lift[48:96, 64:128] = sum_coarse[:, 128:].astype(jnp.bfloat16)
    lift[96:144, :] = sum_coarse[:, :128].astype(jnp.bfloat16)


def side(*args):
    half = jnp.bfloat16
    return pl.pallas_call(
        side_kernel,
        out_shape=[jax.ShapeDtypeStruct(shape, half) for shape in ((256, 128), (256, 128), (144, 128))],
        in_specs=[pl.BlockSpec(memory_space=pl.ANY)] * 10,
        scratch_shapes=[pltpu.VMEM((CELLS, width), half) for width in (256, 128, 128)]
        + [pltpu.VMEM(array.shape, half) for array in args]
        + [pltpu.SemaphoreType.DMA((10,))],
        compiler_params=PARAMS,
        name="side",
    )(*args)


IN_VMEM = pl.BlockSpec(memory_space=pltpu.VMEM)


def near(*arrays):
    return [pltpu.with_memory_space_constraint(array, pltpu.VMEM) for array in arrays]


class Halo:
    def __init__(self, row_0, row_1, col_0, col_1):
        row_parity, col_parity = my_parity()
        row_even, col_even = row_parity == 0, col_parity == 0
        rows, cols = (row_0[...], row_1[...]), (col_0[...], col_1[...])
        self.top, self.bottom = jnp.where(row_even, rows[1], rows[0]), jnp.where(row_even, rows[0], rows[1])
        self.left, self.right = jnp.where(col_even, cols[1], cols[0]), jnp.where(col_even, cols[0], cols[1])


def corner_kernel(row_0, row_1, far_0, far_1, col_0, col_1, side_0, side_1, sems):
    half = jnp.bfloat16
    pull((far_0, far_1), (side_0, side_1), sems)
    row_parity, col_parity = my_parity()
    row_even = row_parity == 0
    halos = (jnp.where(row_even, row_1[...], row_0[...]), jnp.where(row_even, row_0[...], row_1[...]))
    wide = jnp.concatenate(
        [
            jnp.concatenate([jnp.concatenate([rim[576:704, :], rim[768:896, 0:64]], axis=1),
                             jnp.concatenate([rim[704:768, :], rim[768:832, 64:128]], axis=1)], axis=0)
            for rim in halos
        ],
        axis=0,
    )
    sides = []
    for (first, second, single), starts in (((0, 1, 0), (0, 192)), ((126, 127, 127), (96, 240))):
        parts = []
        for rim in halos:
            edge = (
                dot(picks((16, 128), ((0, first), (1, second))), rim[starts[0] : starts[0] + 256], 1, 1)
                + dot(picks((16, 128), ((2, single),)), rim[starts[1] : starts[1] + 256], 1, 1)
                + dot(picks((16, 128), ((3, first), (4, second))), rim[288:544], 1, 1)
                + dot(picks((16, 128), ((5, single),)), rim[480:736], 1, 1)
            ).astype(half)
            parts += [edge[:, :128], edge[:, 128:]]
        first, second, single = (0, 1, 0) if first == 0 else (62, 63, 63)
        pairs = []
        for index, at in ((0, 0), (5, 192)):
            pairs += [(index, at + first), (index + 1, at + second), (index + 2, at + 64 + first), (index + 3, at + 64 + second)]
            pairs.append((index + 4, at + 128 + single))
        rim = dot(picks((16, 384), pairs), wide).astype(half)
        parts += [rim[:, :128], jnp.concatenate([rim[:, 128:], jnp.zeros((16, 64), half)], axis=1)]
        sides.append(jnp.concatenate(parts, axis=0))
    for out, side, to_right in ((col_0, side_0, col_parity == 0), (col_1, side_1, col_parity == 1)):
        out[0:256, :] = side[...]
        out[256:352, :] = jnp.where(to_right, sides[1], sides[0])


def corners(*messages):
    return pl.pallas_call(
        corner_kernel,
        out_shape=[pltpu.VMEM((352, 128), jnp.bfloat16)] * 2,
        out_specs=[IN_VMEM] * 2,
        in_specs=[IN_VMEM] * 2 + [pl.BlockSpec(memory_space=pl.ANY)] * 2,
        scratch_shapes=[pltpu.VMEM((256, 128), jnp.bfloat16)] * 2 + [pltpu.SemaphoreType.DMA((2,))],
        compiler_params=PARAMS,
        name="corners",
    )(*near(*messages[:2]), *messages[2:])


def channel_part(halo, second, refs, write_px, *, chans, rows, width, edge, fill_rows):
    source, inner, px, mx, ix, sx, acc_first, acc_second = refs
    ring = width + 128
    half = jnp.bfloat16

    ix[chans : chans + CELLS, 0:width] = jnp.transpose(inner[...], (1, 0, 2)).reshape(CELLS, width)
    sx[...] = jnp.transpose(source[...], (1, 0, 2)).reshape(CELLS, width)
    fill_rows(mx, ix, halo.top, 0, 0)
    fill_rows(mx, ix, halo.bottom, 2 * chans + CELLS, chans + CELLS)
    place = picks(
        (32, 256),
        ((edge, 0), (edge + 1, 1), (16 + edge, 126), (17 + edge, 127), (edge + 2, 128), (18 + edge, 255)),
    )

    def columns(right, left, tile):
        rows16 = slice(tile * 16, (tile + 1) * 16)
        both = jnp.concatenate([right[rows16, :], left[rows16, :]], axis=0)
        return dot(both, place, 0, 0).astype(half)

    for tile in range(12):
        cols = columns(halo.right, halo.left, tile)
        mx[2 * chans + tile * 128 : 2 * chans + (tile + 1) * 128, width:ring] = cols[:, :128]
        ix[chans + tile * 128 : chans + (tile + 1) * 128, width:ring] = cols[:, 128:]
    for tile in range(-(-2 * chans // 128)):
        size = min(128, 2 * chans - tile * 128)
        for first_tile, at, inner_at in ((16, 0, 0), (18, 2 * chans + CELLS, chans + CELLS)):
            cols = columns(halo.right, halo.left, first_tile + tile)
            mx[at + tile * 128 : at + tile * 128 + size, width:ring] = cols[:size, :128]
            if tile == 0:
                ix[inner_at : inner_at + chans, width:ring] = cols[:chans, 128:]

    def before(row, carry):
        at = pl.multiple_of(row * chans, 16)
        inner_grad = ring_taps(second[...], mx[pl.ds(at, 3 * chans), :], chans, ring)
        px[pl.ds(at, chans), :] = keep(ix[pl.ds(at, chans), :].astype(jnp.float32), inner_grad).astype(half)
        return carry

    lax.fori_loop(0, rows + 2, before, 0, unroll=True)
    write_px()

    def spread(tile):
        wide = jnp.concatenate([tile.astype(jnp.float32), jnp.zeros((chans, 128), jnp.float32)], axis=1)
        return jnp.concatenate([pltpu.roll(wide, 1, 1), wide, pltpu.roll(wide, ring - 1, 1)], axis=0).astype(half)

    acc_first[...] = jnp.zeros(acc_first.shape, jnp.float32)
    acc_second[...] = jnp.zeros(acc_second.shape, jnp.float32)

    def after(row, carry):
        at = pl.multiple_of(row * chans, 16)
        window = px[pl.ds(at, 3 * chans), :]
        acc_first[...] += dot(spread(sx[pl.ds(at, chans), :]), window, 1, 1)
        own = ix[pl.ds(pl.multiple_of(at + chans, 16), chans), 0:width]
        acc_second[...] += dot(spread(own), mx[pl.ds(pl.multiple_of(at + chans, 16), 3 * chans), :], 1, 1)
        return carry

    lax.fori_loop(0, rows, after, 0, unroll=True)


def ring_taps(weight, window, chans, ring):
    parts = dot(weight, window)
    return pltpu.roll(parts[:chans], ring - 1, 1) + parts[chans : 2 * chans] + pltpu.roll(parts[2 * chans :], 1, 1)


def input_kernel(masked, px, raw, out, ox, first, *, chans, rows, width):
    first[...] = stacked_rows(raw, chans)

    def step(row, carry):
        at = pl.multiple_of(row * chans, 16)
        grad = ring_taps(first[...], px[pl.ds(at, 3 * chans), :], chans, width + 128)[:, :width]
        ox[pl.ds(row, 1), :, :] = (masked[pl.ds(at, chans), :].astype(jnp.float32) + grad).astype(jnp.bfloat16)[None]
        return carry

    lax.fori_loop(0, rows, step, 0, unroll=True)
    out[...] = jnp.transpose(ox[...], (1, 0, 2))


def fine_rows(mx, ix, halo, at, inner_at):
    mx[at : at + 96, 0:128] = halo[0:96, :]
    mx[at : at + 96, 128:256] = halo[96:192, :]
    ix[inner_at : inner_at + 48, 0:128] = halo[192:240, :]
    ix[inner_at : inner_at + 48, 128:256] = halo[240:288, :]


def mid_rows(mx, ix, halo, at, inner_at):
    mx[at : at + 192, 0:128] = halo[288:480, :]
    ix[inner_at : inner_at + 96, 0:128] = halo[480:576, :]


def fine_grads(sums, acc_first, acc_second, lift):
    full, half = jnp.float32, jnp.bfloat16
    for index, acc in enumerate((acc_second, acc_first)):
        taps = [acc[:, (2 - tap) * FINE : (3 - tap) * FINE] for tap in range(3)]
        gap = jnp.zeros((144, 16), full)
        sums[index, 0:144, :] = jnp.concatenate([taps[0], gap, taps[1], gap], axis=1).astype(half)
        sums[index, 144:288, :] = jnp.concatenate([taps[2], jnp.zeros((144, 80), full)], axis=1).astype(half)
        sums[index, 288:384, :] = jnp.zeros((96, 128), half)
    sums[0, 288:336, :] = lift[0:48, :]
    sums[1, 288:336, :] = lift[96:144, :]
    sums[1, 144:192, 64:128] = lift[48:96, 64:128]


def mid_grads(sums, acc_first, acc_second):
    for index, acc in enumerate((acc_second, acc_first)):
        for tap in range(3):
            part = jnp.concatenate([acc[:, (2 - tap) * MID : (3 - tap) * MID], jnp.zeros((288, 32), jnp.float32)], axis=1)
            sums[index, tap * 288 : (tap + 1) * 288, :] = part.astype(jnp.bfloat16)


def stacked_rows(weight, chans):
    return jnp.concatenate([weight[tap].reshape(3 * chans, chans) for tap in (2, 1, 0)], axis=1)


def channel_input(masked, px, first, chans, rows, width, name):
    def kernel(*refs):
        input_kernel(*refs, chans=chans, rows=rows, width=width)

    return pl.pallas_call(
        kernel,
        out_shape=jax.ShapeDtypeStruct((chans, rows, width), jnp.bfloat16),
        scratch_shapes=[pltpu.VMEM((rows, chans, width), jnp.bfloat16), pltpu.VMEM((3 * chans, 3 * chans), jnp.bfloat16)],
        compiler_params=PARAMS,
        name=name,
    )(masked, px, first)


def coarse_places():
    place = np.zeros((2, 13 * 16, 96), np.float32)
    for index, first_row, count, sides in ((0, -2, 12, ((0, 0, "r"), (1, 1, "r"), (14, 0, "l"), (15, 1, "l"))), (1, -1, 10, ((0, 2, "r"), (15, 2, "l")))):
        for block in range(count + 1):
            for at, which, side in sides:
                row = first_row + block - (1 if side == "r" else 0)
                if row < first_row or row >= first_row + count:
                    continue
                if 0 <= row < 8:
                    source = (0 if side == "r" else 32) + which * 8 + row
                else:
                    source = (64 if side == "r" else 80) + (0 if row < 0 else 5)
                    source += 4 if index else 2 * (row + 2 if row < 0 else row - 8) + which
                place[index, block * 16 + at, source] = 1
    return place.reshape(2 * 13 * 16, 96)


def coarse_taps(ref, weight, start, size):
    total = jnp.zeros((size, COARSE), jnp.float32)
    for row_tap in range(3):
        for col_tap in range(3):
            at = start + (2 - row_tap) * PITCH
            total += dot(ref[col_tap, at : at + size, :], weight[row_tap, col_tap], 1, 1)
    return total


def coarse_part(halo, second, place, refs, write_px):
    source, inner, masked, sums, px, mx, ix, own, turned = refs
    half = jnp.bfloat16
    lead = 16
    rims = jnp.concatenate(
        [jnp.concatenate([rim[192:224, :], rim[224:256, 0:64]], axis=1) for rim in (halo.right, halo.left)]
        + [jnp.concatenate([rim[320:336, :], rim[336:352, 0:64]], axis=1) for rim in (halo.right, halo.left)],
        axis=0,
    )
    rims = dot(place[...], rims).astype(half)

    def rows_of(rim):
        pair = jnp.concatenate([rim[576:704, :], rim[768:896, 0:64]], axis=1)
        single = jnp.concatenate([rim[704:768, :], rim[768:832, 64:128]], axis=1)
        return pair, single

    above, above_inner = rows_of(halo.top)
    below, below_inner = rows_of(halo.bottom)
    grid = [above[:64], above[64:]] + [masked[k] for k in range(8)] + [below[:64], below[64:]]
    inner_grid = [above_inner] + [inner[k] for k in range(8)] + [below_inner]
    for ref, blocks, at in ((mx.at[1], grid, 0), (ix, inner_grid, 208)):
        ref[0:lead, :] = rims[at : at + 16]
        for k, block in enumerate(blocks):
            start = lead + k * PITCH
            ref[start : start + 64, :] = block
            ref[start + 64 : start + PITCH, :] = rims[at + (k + 1) * 16 : at + (k + 2) * 16]

    def shifted(ref, size):
        whole = ref[1].astype(jnp.float32)
        ref[0] = pltpu.roll(whole, size - 1, 0).astype(half)
        ref[2] = pltpu.roll(whole, 1, 0).astype(half)

    shifted(mx, 976)
    for start in range(0, 816, 272):
        inner_grad = coarse_taps(mx, second, start, 272)
        px[1, start : start + 272, :] = keep(
            ix[start : start + 272, :].astype(jnp.float32), inner_grad
        ).astype(half)
    shifted(px, 816)
    write_px()
    def corr(tile, ref, start, write):
        own[...] = jnp.zeros(own.shape, half)
        for row in range(8):
            own[row * PITCH : row * PITCH + 64, :] = tile[row]
        turned[...] = jnp.transpose(own[...].astype(jnp.float32)).astype(half)
        for row_tap in range(3):
            for col_tap in range(3):
                at = start + (2 - row_tap) * PITCH
                write(row_tap * 3 + col_tap, dot(turned[...], ref[col_tap, at : at + 8 * PITCH, :]))

    def writer(index):
        def write(tap, value):
            sums[index, tap * COARSE : (tap + 1) * COARSE, :] = value[:, :128].astype(half)
            tail = jnp.concatenate([value[:96, 128:], value[96:, 128:]], axis=1)
            sums[index, AT_TAIL + tap * 96 : AT_TAIL + (tap + 1) * 96, :] = tail.astype(half)

        return write

    corr(inner, mx, lead + PITCH, writer(0))
    corr(source, px, lead, writer(1))


def grads_kernel(*refs):
    messages, weights, refs = refs[:4], refs[4:9], refs[9:]
    arrays, (px_coarse, px_mid, px_fine, kept, given), refs = refs[:9], refs[9:14], refs[14:]
    held, work, refs = refs[:7], refs[7:27], refs[27:]
    (second_coarse, raw_mid, raw_fine, place, lift, second_mid, second_fine), (load_sems, px_sems, sum_sems) = refs[:7], refs[7:]
    coarse_work, mid_work, fine_work = work[:6], work[6:13], work[13:20]
    sum_coarse, sum_mid, sum_fine = coarse_work[0], mid_work[0], fine_work[0]
    mx_mid, mx_fine = mid_work[2], fine_work[2]
    core, _ = my_parity()

    places = (
        *held[:3], second_coarse, place,
        held[3], held[4], mx_mid.at[2 * MID : 2 * MID + CELLS, 0:128], raw_mid,
        held[5], held[6], mx_fine.at[2 * FINE : 2 * FINE + CELLS, 0:256], raw_fine, lift,
    )
    arrays = (
        *arrays[:3], weights[0], weights[3], *arrays[3:6], weights[1], *arrays[6:], weights[2], weights[4],
    )
    loads = [pltpu.make_async_copy(array, to, load_sems.at[k]) for k, (array, to) in enumerate(zip(arrays, places))]
    for load in loads:
        load.start()
    halo = Halo(*messages)

    px_copies = [
        pltpu.make_async_copy(work[1], out, px_sems.at[k])
        for k, (work, out) in enumerate(((coarse_work, px_coarse), (mid_work, px_mid), (fine_work, px_fine)))
    ]
    def sum_copies(work, start, size, k):
        return [
            [pltpu.make_async_copy(work.at[half], out.at[start : start + size, :], sum_sems.at[2 * k + half]) for out in (kept, given)]
            for half in range(2)
        ]

    def write(copies):
        for half in range(2):
            keeps = core == half

            @pl.when(keeps)
            def _(half=half):
                copies[half][0].start()

            @pl.when(jnp.logical_not(keeps))
            def _(half=half):
                copies[half][1].start()

    pieces = ((sum_coarse, 0, AT_MID), (sum_mid, AT_MID, AT_FINE - AT_MID), (sum_fine, AT_FINE, HALF_ROWS - AT_FINE))
    sums = [sum_copies(*piece, k) for k, piece in enumerate(pieces)]

    for load in loads[:5]:
        load.wait()
    coarse_part(halo, second_coarse, place, (*held[:3], *coarse_work), px_copies[0].start)
    write(sums[0])

    for load in loads[5:9]:
        load.wait()
    second_mid[...] = stacked_rows(raw_mid, MID)
    channel_part(
        halo, second_mid, (held[3], held[4], *mid_work[1:]), px_copies[1].start,
        chans=MID, rows=16, width=128, edge=3, fill_rows=mid_rows,
    )
    mid_grads(sum_mid, mid_work[5], mid_work[6])
    write(sums[1])

    for load in loads[9:]:
        load.wait()
    second_fine[...] = stacked_rows(raw_fine, FINE)
    channel_part(
        halo, second_fine, (held[5], held[6], *fine_work[1:]), px_copies[2].start,
        chans=FINE, rows=32, width=256, edge=0, fill_rows=fine_rows,
    )
    fine_grads(sum_fine, fine_work[5], fine_work[6], lift)
    write(sums[2])

    for copy in px_copies:
        copy.wait()
    for halves in sums:
        for copies in halves:
            copies[0].wait()


def grads(messages, seconds, lift, arrays):
    half = jnp.bfloat16
    any_memory = pl.BlockSpec(memory_space=pl.ANY)
    full = jnp.float32

    def channel_work(chans, rows, width, sum_rows):
        ring = width + 128
        return [
            ((2, sum_rows, 128), half),
            (((rows + 2) * chans, ring), half),
            (((rows + 4) * chans, ring), half),
            (((rows + 2) * chans, ring), half),
            ((CELLS, width), half),
            ((3 * chans, 3 * chans), full),
            ((3 * chans, 3 * chans), full),
        ]

    tile = ((COARSE_ROWS, COARSE_COLS, COARSE), half)
    held = [tile, tile, tile] + [((MID, 16, 128), half)] * 2 + [((FINE, 32, 256), half)] * 2
    coarse_work = [
        ((2, AT_MID, 128), half),
        ((3, 816, COARSE), half),
        ((3, 976, COARSE), half),
        ((816, COARSE), half),
        ((8 * PITCH, COARSE), half),
        ((COARSE, 8 * PITCH), half),
    ]
    scratch = held + coarse_work + channel_work(MID, 16, 128, AT_FINE - AT_MID) + channel_work(FINE, 32, 256, HALF_ROWS - AT_FINE)
    shapes = (
        (3, 3, COARSE, COARSE), (3, 3, MID, MID), (3, 3, FINE, FINE), (2 * 13 * 16, 96), (144, 128),
        (3 * MID, 3 * MID), (3 * FINE, 3 * FINE),
    )
    weights = [(shape, half) for shape in shapes]
    return pl.pallas_call(
        grads_kernel,
        out_shape=[
            jax.ShapeDtypeStruct((3, 816, COARSE), half),
            jax.ShapeDtypeStruct((18 * MID, 256), half),
            jax.ShapeDtypeStruct((34 * FINE, 384), half),
            jax.ShapeDtypeStruct((HALF_ROWS, 128), half),
            pltpu.VMEM((HALF_ROWS, 128), half),
        ],
        in_specs=[IN_VMEM] * 4 + [any_memory] * 14,
        out_specs=[any_memory] * 4 + [IN_VMEM],
        scratch_shapes=[pltpu.VMEM(*shape) for shape in scratch + weights]
        + [pltpu.SemaphoreType.DMA((14,)), pltpu.SemaphoreType.DMA((3,)), pltpu.SemaphoreType.DMA((6,))],
        compiler_params=PARAMS,
        name="grads",
    )(*near(*messages), *seconds, jnp.asarray(coarse_places(), half), lift, *arrays)


def coarse_input_kernel(masked, px, first, out):
    for start in range(0, 8, 4):
        grad = coarse_taps(px, first, 16 + start * PITCH, 4 * PITCH)
        for row in range(start, start + 4):
            at = (row - start) * PITCH
            out[row] = (masked[row].astype(jnp.float32) + grad[at : at + 64]).astype(jnp.bfloat16)


def coarse_input(masked, px, first):
    return pl.pallas_call(
        coarse_input_kernel,
        out_shape=jax.ShapeDtypeStruct((COARSE_ROWS, COARSE_COLS, COARSE), jnp.bfloat16),
        compiler_params=PARAMS,
        name="coarse_input",
    )(masked, px, first)


def unpack_kernel(summed, *refs, kept):
    outs, (coarse, mid, fine, lift_mid, lift_coarse, sems) = refs[-14:-6], refs[-6:]
    core, _ = my_parity()
    is_second = core == (0 if kept else 1)
    full = jnp.float32
    copies = []

    def leave(tile, first_out, second_out):
        k = len(copies)
        copies.append(pltpu.make_async_copy(tile, second_out, sems.at[k]))
        other = pltpu.make_async_copy(tile, first_out, sems.at[k])

        @pl.when(is_second)
        def _():
            copies[k].start()

        @pl.when(jnp.logical_not(is_second))
        def _():
            other.start()

    for tap in range(9):
        row_tap, col_tap = tap // 3, tap % 3
        coarse[row_tap, col_tap, :, 0:128] = summed[tap * COARSE : (tap + 1) * COARSE, :].astype(full)
        tail = summed[AT_TAIL + tap * 96 : AT_TAIL + (tap + 1) * 96, :].astype(full)
        coarse[row_tap, col_tap, 0:96, 128:192] = tail[:, :64]
        coarse[row_tap, col_tap, 96:192, 128:192] = tail[:, 64:]
        if col_tap == 2:
            leave(coarse.at[row_tap], outs[4].at[row_tap], outs[5].at[row_tap])
    for tap in range(9):
        mid[tap // 3, tap % 3] = summed[AT_MID + tap * MID : AT_MID + (tap + 1) * MID, 0:96].astype(full)
    leave(mid, outs[2], outs[3])
    for col_tap in range(3):
        rows = slice(AT_FINE + col_tap * FINE, AT_FINE + (col_tap + 1) * FINE)
        pair = summed[rows, :].astype(full)
        fine[0, col_tap] = pair[:, 0:48]
        fine[1, col_tap] = pair[:, 64:112]
        rows = slice(AT_FINE + 144 + col_tap * FINE, AT_FINE + 144 + (col_tap + 1) * FINE)
        fine[2, col_tap] = summed[rows, 0:48].astype(full)
    leave(fine, outs[0], outs[1])
    lift_mid[...] = summed[AT_LIFT : AT_LIFT + 48, 0:96].astype(full)
    lift_coarse[:, 0:128] = summed[AT_LIFT : AT_LIFT + 48, :].astype(full)
    lift_coarse[:, 128:192] = summed[AT_FINE + 144 : AT_FINE + 192, 64:128].astype(full)
    lift_copies = [
        pltpu.make_async_copy(tile, out, sems.at[len(copies)]) for tile, out in ((lift_mid, outs[6]), (lift_coarse, outs[7]))
    ]

    @pl.when(is_second)
    def _():
        lift_copies[0].start()
        lift_copies[0].wait()

    @pl.when(jnp.logical_not(is_second))
    def _():
        lift_copies[1].start()
        lift_copies[1].wait()

    for copy in copies:
        copy.wait()


def unpack(summed, earlier=()):
    shapes = ((3, 3, 48, 48),) * 2 + ((3, 3, 96, 96),) * 2 + ((3, 3, 192, 192),) * 2 + ((48, 96), (48, 192))
    any_memory = pl.BlockSpec(memory_space=pl.ANY)

    def kernel(*refs):
        unpack_kernel(*refs, kept=not earlier)

    return pl.pallas_call(
        kernel,
        out_shape=[jax.ShapeDtypeStruct(shape, jnp.float32) for shape in shapes],
        in_specs=[IN_VMEM] + [any_memory] * len(earlier),
        out_specs=[any_memory] * 8,
        scratch_shapes=[pltpu.VMEM(shapes[k], jnp.float32) for k in (4, 2, 0, 6, 7)] + [pltpu.SemaphoreType.DMA((6,))],
        input_output_aliases={k + 1: k for k in range(len(earlier))},
        compiler_params=PARAMS,
        name="unpack_other" if earlier else "unpack_kept",
    )(*near(summed), *earlier)


def on_device(
    grad_joined, joined_fine, input_fine, inner_fine, unit_fine, input_mid, inner_mid, unit_mid,
    input_coarse, inner_coarse, unit_coarse, first_fine, second_fine, first_mid, second_mid,
    first_coarse, second_coarse, lift_mid, lift_coarse,
):
    input_coarse, inner_coarse, unit_coarse = (
        jnp.transpose(x, (1, 2, 0)) for x in (input_coarse, inner_coarse, unit_coarse)
    )
    fine, mid, coarse, row_0, row_1, pooled_mid, pooled_coarse = prep(
        grad_joined, joined_fine, unit_fine, inner_fine, unit_mid, inner_mid, unit_coarse, inner_coarse,
        jnp.transpose(lift_mid), jnp.transpose(lift_coarse),
    )
    row_0, row_1 = send(row_0, swap_pairs(0, None)), send(row_1, swap_pairs(1, None))
    side_0, side_1, lift = side(
        fine, mid, coarse, inner_fine, inner_mid, inner_coarse, unit_mid, unit_coarse, pooled_mid, pooled_coarse
    )
    col_0, col_1 = corners(row_0, row_1, side_0, side_1)
    col_0, col_1 = send(col_0, swap_pairs(None, 0)), send(col_1, swap_pairs(None, 1))
    coarse_px, mid_px, fine_px, kept, given = grads(
        (row_0, row_1, col_0, col_1),
        (second_coarse, second_mid, second_fine),
        lift,
        (input_coarse, inner_coarse, coarse, input_mid, inner_mid, mid, input_fine, inner_fine, fine),
    )
    other, earlier, fine_input, mid_input, input_grad = all_sum(
        kept,
        given,
        (
            (lambda px: channel_input(fine, px, first_fine, FINE, 32, 256, "fine_input"), fine_px),
            (lambda px: channel_input(mid, px, first_mid, MID, 16, 128, "mid_input"), mid_px),
            (lambda px: coarse_input(coarse, px, first_coarse), coarse_px),
        ),
        unpack,
    )
    *taps, lift_mid, lift_coarse = unpack(other, earlier)
    return (
        fine_input, mid_input, jnp.transpose(input_grad, (2, 0, 1)), *taps, jnp.transpose(lift_mid), jnp.transpose(lift_coarse)
    )


def solution(mesh):
    tiled = P(None, "row", "col")
    return jax.shard_map(
        on_device,
        mesh=mesh,
        in_specs=(tiled,) * 11 + (P(),) * 8,
        out_specs=(tiled,) * 3 + (P(),) * 8,
        check_vma=False,
    )
```
